32 devices in a mesh: row: 8 (over y, x, core), col: 4 (over z).
Axes of the slice: x: 2, y: 2, z: 4, core: 2. Of those that a mesh axis runs over, the one named last changes fastest.
Arguments:
- inverse_block: float32 [16384, 16384], P('row', 'col'), may hold values from -6 to 6
- tile_list: int32 [32], replicated, may hold values from 0 to 63, as said below
- panels: bfloat16 [3, 16384, 512], P(None, 'row'), may hold values from -0.0625 to 0.0625
- links: bfloat16 [2, 512, 512], P(None, 'col'), may hold values from -0.25 to 0.25
- diag_inverse: float32 [3, 512, 512], P(None, None, 'col'), may hold values from -6 to 6
Outputs:
- panel_inverse: float32 [3, 16384, 512], P(None, 'row', 'col')
- cross_inverse: float32 [2, 512, 512], P(None, None, 'col')
- diag_block: float32 [3, 512, 512], P(None, None, 'col')
The draws below stay inside these ranges and needn't reach their ends.
Inputs may be any that keep to these rules, and one draw needn't show every extreme that they name: `tile_list`: 32 different tile numbers in ascending order; for each g from 0 to 4 - 1, the aligned group of tiles g * (64 // 4) to (g + 1) * (64 // 4) - 1 holds at least one of them.
All inputs are finite; a program needn't handle non-finite values.
Results may differ from the reference program's by a relative error of at most 0.0003.
Values may be sent and summed in bfloat16 or wider, within the bound.
No kernel may reach another device: no remote copies, remote signals or barrier semaphores. Data moves between devices by JAX's collectives and lax.ppermute only.
A program may use at most 128 MiB of HBM per device.

```python
import jax
import jax.numpy as jnp
from jax import lax

ORDER = 16384
TILE = 256
W = 512
LIST = 32
SUPER = 3
N_COL = 4


def draw_tile_list(key, part):
    tile_count = ORDER // TILE
    group = tile_count // N_COL
    key_heat, key_noise, key_first, key_order = jax.random.split(jax.random.fold_in(key, 11), 4)
    heat = jax.random.randint(key_heat, (N_COL,), 0, 4)
    places = jnp.arange(tile_count, dtype=jnp.int32)
    owners = places // group
    noise = jax.random.randint(key_noise, (tile_count,), 0, 4)
    first = jax.random.randint(key_first, (N_COL,), 0, group)
    forced = places % group == first[owners]
    scores = jnp.where(forced, 1000, noise + 3 * heat[owners])
    order = jax.random.permutation(key_order, tile_count)
    totals = scores * tile_count + order
    chosen = lax.top_k(totals, LIST)[1]
    return jnp.sort(chosen).astype(jnp.int32)


def levels(stream_key, shape, pieces, smallest, largest):
    loudness, own = 1.0, jax.random.fold_in(stream_key, 6)
    for dim, blocks in pieces:
        heights = jnp.exp(jax.random.uniform(jax.random.fold_in(own, dim), (blocks,), jnp.float32, smallest / len(pieces), largest / len(pieces)))
        loudness = loudness * jnp.repeat(heights, shape[dim] // blocks).reshape([-1 if axis == dim else 1 for axis in range(len(shape))])
    return loudness


def gaussian(own_key, shape, spread, limit, cuts=(), kind=jnp.bfloat16):
    entries = jax.random.normal(own_key, shape, jnp.float32) * spread
    if len(cuts) > 0:
        entries = levels(own_key, shape, cuts, -0.22, 0.18) * entries
    return jnp.clip(entries, min=-limit, max=limit).astype(kind)


def setup_inputs(seed: int = 0) -> dict:
    seeds = jax.random.split(jax.random.key(seed), 6)
    inverse_block = gaussian(seeds[0], (ORDER, ORDER), 1.0, 6.0, ((0, 8), (1, 4)), jnp.float32)
    tile_list = draw_tile_list(jax.random.fold_in(seeds[5], 71), 0)
    panels = gaussian(seeds[2], (SUPER, ORDER, W), (LIST * TILE) ** -0.5, 0.0625, ((1, 8),))
    links = gaussian(seeds[3], (SUPER - 1, W, W), W ** -0.5, 0.25, ((1, 4),))
    diag_inverse = gaussian(seeds[4], (SUPER, W, W), 1.0, 6.0, ((2, 4),), jnp.float32)
    return {"inverse_block": inverse_block, "tile_list": tile_list, "panels": panels, "links": links, "diag_inverse": diag_inverse}


precise = lax.Precision.HIGHEST


def product(left, right):
    return jnp.dot(left, right, precision=precise, preferred_element_type=jnp.float32)


def reference(inverse_block, tile_list, panels, links, diag_inverse):
    offsets = jnp.arange(TILE, dtype=jnp.int32)
    row_index = (tile_list[:, None].astype(jnp.int32) * TILE + offsets[None, :]).reshape(-1).astype(jnp.int32)
    resident = jnp.take(jnp.take(inverse_block, row_index, axis=0), row_index, axis=1)
    panel_list = []
    cross_list = []
    diag_list = []
    previous = None
    diag_prev = None
    for supernode in range(SUPER):
        factor = jnp.take(panels[supernode], row_index, axis=0).astype(jnp.float32)
        inner_sum = product(resident, factor)
        if supernode > 0:
            link_block = links[supernode - 1].astype(jnp.float32)
            inner_sum = inner_sum + product(previous, link_block)
            cross_block = -(product(previous.T, factor) + product(diag_prev, link_block))
        current = -inner_sum
        diag_now = diag_inverse[supernode] - product(factor.T, current)
        if supernode > 0:
            diag_now = diag_now - product(link_block.T, cross_block)
            cross_list.append(cross_block)
        full_panel = jnp.zeros((ORDER, W), jnp.float32).at[row_index].set(current)
        panel_list.append(full_panel)
        diag_list.append(diag_now)
        previous = current
        diag_prev = diag_now
    return jnp.stack(panel_list), jnp.stack(cross_list), jnp.stack(diag_list)
```

```python
import functools

import jax
import jax.numpy as jnp
from jax import lax
from jax.experimental import pallas as pl
from jax.experimental.pallas import tpu as pltpu
from jax.sharding import PartitionSpec as P

ORDER = 16384
TILE = 256
PAD = 16

precise = lax.Precision.HIGHEST
f32 = jnp.float32
bf16 = jnp.bfloat16
BOTH = ("row", "col")


def product(left, right):
    return jnp.dot(left, right, precision=precise, preferred_element_type=f32)


def split(value):
    high = value.astype(bf16)
    return high, (value - high.astype(f32)).astype(bf16)


def split_dot(value, right):
    high, low = split(value)
    return jnp.dot(high, right, preferred_element_type=f32) + jnp.dot(
        low, right, preferred_element_type=f32
    )


def shift(value, by, size):
    return lax.ppermute(value, "col", [(z, (z + by) % size) for z in range(size)])


def swap(value, bit, size):
    return lax.ppermute(value, "row", [(r, r ^ bit) for r in range(size)])


def messages_of(rows, cols):
    tiles = rows // TILE
    out = []
    for by in range(1, cols):
        if 2 * by == cols and tiles % 2 == 0:
            out += [(by, 0, rows // 2), (by, rows // 2, rows // 2)]
        else:
            out.append((by, 0, rows))
    return out


def panel_kernel(plan, first, last, meta, s_ref, own_ref, oth_ref, *rest):
    cols, pieces, messages = plan
    rest = list(rest)
    if not first:
        link_ref, prev_ref = rest[:2]
        rest = rest[2:]
    part_ref = None
    if not last:
        part_ref = rest.pop(0)
    mine_ref = rest.pop(0)
    out_refs = rest[: len(messages)]
    p_ref, exp_ref, sem = rest[len(messages) :]
    step = pl.program_id(0)
    group = own_ref.shape[0]
    piece = group // pieces
    width = p_ref.shape[1]
    share = width // cols
    lane, start, col = meta[0], meta[1], meta[2]

    def copies():
        found = []
        for half, ref in ((lane, own_ref), (1 - lane, oth_ref)):
            for j in range(pieces):
                at = half * group + lax.rem(start + j, pieces) * piece
                found.append(
                    pltpu.make_async_copy(
                        ref.at[pl.ds(j * piece, piece)],
                        p_ref.at[pl.ds(pl.multiple_of(at, piece), piece)],
                        sem,
                    )
                )
        return found

    @pl.when(step == 0)
    def _():
        exp_ref[...] = jnp.zeros_like(exp_ref)
        for copy in copies():
            copy.start()
        for copy in copies():
            copy.wait()

    def emit(value):
        if value is None:
            quant = jnp.zeros((TILE, width), jnp.int16)
            power = jnp.zeros((1, width), jnp.int16)
        else:
            top = jnp.max(jnp.abs(value), axis=0, keepdims=True)
            expo = jnp.clip(jnp.ceil(jnp.log2(jnp.maximum(top, 1e-30))), -100.0, 100.0)
            scaled = jnp.round(value * jnp.exp2(15.0 - expo))
            quant = jnp.clip(scaled, -32767.0, 32767.0).astype(jnp.int32).astype(jnp.int16)
            power = expo.astype(jnp.int32).astype(jnp.int16)
        if part_ref is not None:
            part_ref[...] = jnp.zeros((TILE, width), f32) if value is None else value
        for here in range(cols):

            @pl.when(col == here)
            def _(here=here):
                mine = slice(here * share, (here + 1) * share)
                mine_ref[...] = (
                    jnp.zeros((TILE, share), f32) if value is None else value[:, mine]
                )
                for (by, row, count), ref in zip(messages, out_refs):
                    to = (here + by) % cols
                    chunk = slice(to * share, (to + 1) * share)
                    at = step * TILE - row

                    @pl.when((at >= 0) & (at < count))
                    def _():
                        ref[pl.ds(pl.multiple_of(at, TILE), TILE), :] = quant[:, chunk]

        spot = lax.broadcasted_iota(jnp.int32, exp_ref.shape, 0) == step
        exp_ref[...] = jnp.where(
            spot, jnp.broadcast_to(power.astype(jnp.int32), exp_ref.shape), exp_ref[...]
        )

    listed = meta[3 + step] > 0

    @pl.when(listed)
    def _():
        total = split_dot(s_ref[...], p_ref[...])
        if not first:
            total = total + split_dot(prev_ref[...], link_ref[...])
        emit(-total)

    @pl.when(jnp.logical_not(listed))
    def _():
        emit(None)

    @pl.when(step == pl.num_programs(0) - 1)
    def _():
        powers = exp_ref[...].astype(jnp.int16)
        for here in range(cols):

            @pl.when(col == here)
            def _(here=here):
                for (by, row, count), ref in zip(messages, out_refs):
                    to = (here + by) % cols
                    ref[count : count + PAD, :] = powers[:, to * share : (to + 1) * share]


def panel_call(plan, meta, inverse_block, own, oth, link, prev, last):
    cols, pieces, messages = plan
    rows, depth = inverse_block.shape
    width = own.shape[1]
    share = width // cols
    first = link is None
    whole = lambda i, m: (0, 0)
    by_tile = lambda i, m: (i, 0)
    in_specs = [
        pl.BlockSpec((TILE, depth), by_tile),
        pl.BlockSpec(memory_space=pl.ANY),
        pl.BlockSpec(memory_space=pl.ANY),
    ]
    operands = [inverse_block, own, oth]
    if not first:
        in_specs += [pl.BlockSpec((width, width), whole), pl.BlockSpec((TILE, width), by_tile)]
        operands += [link, prev]
    out_specs, out_shape = [], []
    if not last:
        out_specs.append(pl.BlockSpec((TILE, width), by_tile))
        out_shape.append(jax.ShapeDtypeStruct((rows, width), f32))
    out_specs.append(pl.BlockSpec((TILE, share), by_tile))
    out_shape.append(jax.ShapeDtypeStruct((rows, share), f32))
    for _, _, count in messages:
        out_specs.append(pl.BlockSpec((count + PAD, share), whole))
        out_shape.append(jax.ShapeDtypeStruct((count + PAD, share), jnp.int16))
    return pl.pallas_call(
        functools.partial(panel_kernel, plan, first, last),
        grid_spec=pltpu.PrefetchScalarGridSpec(
            num_scalar_prefetch=1,
            grid=(rows // TILE,),
            in_specs=in_specs,
            out_specs=out_specs,
            scratch_shapes=[
                pltpu.VMEM((depth, width), bf16),
                pltpu.VMEM((PAD, width), jnp.int32),
                pltpu.SemaphoreType.DMA,
            ],
        ),
        out_shape=out_shape,
        compiler_params=pltpu.CompilerParams(vmem_limit_bytes=40 << 20),
        cost_estimate=pl.CostEstimate(
            flops=4 * rows * depth * width, bytes_accessed=4 * rows * depth, transcendentals=0
        ),
    )(meta, *operands)


def sum_kernel(messages, mine_ref, *rest):
    out_ref = rest[-1]
    tiles = mine_ref.shape[0] // TILE
    for tile in range(tiles):
        rows = slice(tile * TILE, (tile + 1) * TILE)
        total = mine_ref[rows, :]
        for (_, row, count), ref in zip(messages, rest[:-1]):
            at = tile * TILE - row
            if 0 <= at < count:
                powers = ref[count : count + PAD, :].astype(jnp.int32).astype(f32)
                scale = jnp.exp2(powers[tile : tile + 1, :] - 15.0)
                total = total + ref[at : at + TILE, :].astype(jnp.int32).astype(f32) * scale
        out_ref[rows, :] = total


def sum_call(messages, mine, received):
    return pl.pallas_call(
        functools.partial(sum_kernel, messages),
        out_shape=jax.ShapeDtypeStruct(mine.shape, f32),
        compiler_params=pltpu.CompilerParams(vmem_limit_bytes=24 << 20),
    )(mine, *received)


def around(pieces, col_number):
    size = len(pieces)
    ring = jnp.stack(pieces[::-1] + pieces[:0:-1])
    return lax.dynamic_slice_in_dim(ring, size - 1 - col_number, size, 0)


def row_sum_half(value, lane, row_size):
    half = value.shape[0] // 2
    keep = lax.dynamic_slice_in_dim(value, lane * half, half, 0)
    give = lax.dynamic_slice_in_dim(value, (1 - lane) * half, half, 0)
    keep = keep + swap(give, 1, row_size)
    bit = 2
    while bit < row_size:
        keep = keep + swap(keep, bit, row_size)
        bit *= 2
    return keep


def both_halves(half, lane, row_size):
    other = swap(half, 1, row_size)
    pick = lane == 0
    return jnp.where(pick, half, other), jnp.where(pick, other, half)


def local(inverse_block, tile_list, panels, links, diag_inverse):
    rows_here = inverse_block.shape[0]
    share = diag_inverse.shape[2]
    row_size, col_size = lax.axis_size("row"), lax.axis_size("col")
    row_number, col_number = lax.axis_index("row"), lax.axis_index("col")
    place, lane = row_number // 2, row_number % 2
    supernodes, _, width = panels.shape
    tiles_here = rows_here // TILE
    tiles = row_number * tiles_here + jnp.arange(tiles_here, dtype=jnp.int32)
    flags = jnp.any(tile_list[None, :] == tiles[:, None], axis=1)
    row_mask = jnp.broadcast_to(flags[:, None], (tiles_here, TILE)).reshape(-1, 1)

    pieces = col_size
    piece = rows_here // pieces
    away = (col_number - place) % col_size
    start = (place - col_number) % col_size
    sent_mask = lax.dynamic_slice_in_dim(row_mask, away * piece, piece, 0)
    sent = jnp.where(
        sent_mask[None],
        lax.dynamic_slice_in_dim(panels, away * piece, piece, 1),
        jnp.zeros((), bf16),
    )

    def gather(k):
        got = []
        for j in range(pieces):
            pairs = []
            for c in range(col_size):
                for d in range(col_size):
                    rel = (d - j) % col_size
                    if rel == 0:
                        continue
                    to = (c + rel) % col_size
                    for i in range(2):
                        pairs.append(
                            ((c * 2 + i) * col_size + (c + d) % col_size, (to * 2 + i) * col_size + c)
                        )
            got.append(lax.ppermute(sent[k], BOTH, pairs))
        own = jnp.where(
            start == 0,
            jnp.where(row_mask, panels[k], jnp.zeros((), bf16)),
            jnp.concatenate(got, axis=0),
        )
        return own, swap(own, 1, row_size)

    gathered = [gather(k) for k in range(supernodes)]

    flat = links.reshape(-1, width)
    half = flat.shape[0] // 2
    my_links = lax.dynamic_slice_in_dim(flat, lane * half, half, 0)
    got = around([my_links] + [shift(my_links, s, col_size) for s in range(1, col_size)], col_number)
    low, high = both_halves(got, lane, row_size)
    link_full = jnp.concatenate([low, high], axis=1)
    link_full = link_full.reshape(col_size, supernodes - 1, -1, width)
    link_full = link_full.transpose(1, 0, 2, 3).reshape(supernodes - 1, width, width)

    messages = messages_of(rows_here, col_size)
    plan = (col_size, pieces, messages)
    meta = jnp.concatenate(
        [jnp.stack([lane, start, col_number]), flags.astype(jnp.int32)]
    ).astype(jnp.int32)

    panel_parts, cross_parts, diag_parts = [], [], []
    part = None
    full_diag = None
    turned = None
    for k in range(supernodes):
        last = k + 1 == supernodes
        own, oth = gathered[k]
        found = panel_call(
            plan, meta, inverse_block, own, oth, None if k == 0 else link_full[k - 1], part, last
        )
        if not last:
            part = found[0]
            found = found[1:]
        mine, out = found[0], found[1:]
        received = [None] * len(messages)
        for n, (by, row, count) in enumerate(messages):
            if 2 * by == col_size and count < rows_here:
                step = 1 if row == 0 else -1
                value = out[n]
                for _ in range(by):
                    value = shift(value, step, col_size)
                received[n] = value
        for n, (by, row, count) in enumerate(messages):
            if received[n] is None:
                received[n] = shift(out[n], by, col_size)
        current = sum_call(messages, mine, received)
        panel_parts.append(current)

        factors = [panels[k]] if last else [panels[k], panels[k + 1]]
        sums = jnp.concatenate([product(f.astype(f32).T, current) for f in factors], axis=0)
        sums = sums.reshape(len(factors), 2, width // 2, share).transpose(1, 0, 2, 3)
        summed = row_sum_half(sums.reshape(-1, share), lane, row_size)
        low, high = both_halves(summed, lane, row_size)
        blocks = jnp.stack([low, high]).reshape(2, len(factors), width // 2, share)
        blocks = blocks.transpose(1, 0, 2, 3).reshape(len(factors), width, share)
        diag_now = diag_inverse[k] - blocks[0]
        if k > 0:
            link = link_full[k - 1].astype(f32)
            link_share = lax.dynamic_slice_in_dim(link, col_number * share, share, 1)
            cross = -(turned + product(full_diag, link_share))
            diag_now = diag_now - product(link.T, cross)
            cross_parts.append(cross)
        diag_parts.append(diag_now)
        if not last:
            rest = blocks[1].reshape(col_size, share, share)
            arrived = []
            for s in range(col_size):
                block = lax.dynamic_index_in_dim(rest, (col_number + s) % col_size, 0, False)
                sent_now = jnp.concatenate([diag_now, block], axis=0)
                arrived.append(shift(sent_now, s, col_size) if s else sent_now)
            ordered = around(arrived, col_number)
            full_diag = ordered[:, :width].transpose(1, 0, 2).reshape(width, width)
            turned = ordered[:, width:].transpose(0, 2, 1).reshape(width, share)
    return jnp.stack(panel_parts), jnp.stack(cross_parts), jnp.stack(diag_parts)


def solution(mesh):
    in_specs = (
        P("row", "col"),
        P(),
        P(None, "row", None),
        P(None, "col", None),
        P(None, None, "col"),
    )
    out_specs = (P(None, "row", "col"), P(None, None, "col"), P(None, None, "col"))
    return jax.shard_map(local, mesh=mesh, in_specs=in_specs, out_specs=out_specs, check_vma=False)
```

```python
import functools

import jax
import jax.numpy as jnp
from jax import lax
from jax.experimental import pallas as pl
from jax.experimental.pallas import tpu as pltpu
from jax.sharding import PartitionSpec as P

TILE = 256
PAD = 16
LANES = 2
STREAMS = 2

precise = lax.Precision.HIGHEST
f32 = jnp.float32
bf16 = jnp.bfloat16
i16 = jnp.int16
BOTH = ("row", "col")


def product(left, right):
    return jnp.dot(left, right, precision=precise, preferred_element_type=f32)


def turned_product(left, right):
    return lax.dot_general(
        left, right, (((0,), (0,)), ((), ())), precision=precise, preferred_element_type=f32
    )


def split_dot(value, right):
    high = value.astype(bf16)
    low = (value - high.astype(f32)).astype(bf16)
    return jnp.dot(high, right, preferred_element_type=f32) + jnp.dot(
        low, right, preferred_element_type=f32
    )


def shift(value, by, size):
    return lax.ppermute(value, "col", [(z, (z + by) % size) for z in range(size)])


def swap(value, bit, size):
    return lax.ppermute(value, "row", [(r, r ^ bit) for r in range(size)])


def quantize(value):
    top = jnp.max(jnp.abs(value), axis=0, keepdims=True)
    power = jnp.clip(jnp.ceil(jnp.log2(jnp.maximum(top, 1e-30))), -100.0, 100.0)
    scaled = jnp.clip(jnp.round(value * jnp.exp2(15.0 - power)), -32767.0, 32767.0)
    return scaled.astype(jnp.int32).astype(i16), power.astype(jnp.int32)


def restore(ref, at, tile):
    count = ref.shape[0] - PAD
    powers = ref[count:, :].astype(jnp.int32).astype(f32)
    scale = jnp.exp2(powers[tile : tile + 1, :] - 15.0)
    return ref[at : at + TILE, :].astype(jnp.int32).astype(f32) * scale


def first_kernel(meta, s_own, s_oth, own, oth, total):
    @pl.when(meta[2 + pl.program_id(0)] > 0)
    def _():
        total[...] = split_dot(s_own[...], own[...]) + split_dot(s_oth[...], oth[...])


def second_kernel(cols, chained, meta, s_own, s_oth, own, oth, before, *rest):
    rest = list(rest)
    if chained:
        link, prev = rest[:2]
        rest = rest[2:]
    part, out_a, out_b, powers = rest
    step = pl.program_id(0)
    tiles = pl.num_programs(0)
    share = part.shape[2]
    half = out_a.shape[0] - PAD
    far = lax.rem(meta[1] + cols // 2, cols)

    @pl.when(step == 0)
    def _():
        powers[...] = jnp.zeros_like(powers)

    def put(quant):
        at = step * TILE

        @pl.when(at < half)
        def _():
            out_a[pl.ds(pl.multiple_of(at, TILE), TILE), :] = quant

        @pl.when(at >= half)
        def _():
            out_b[pl.ds(pl.multiple_of(at - half, TILE), TILE), :] = quant

    listed = meta[2 + step] > 0

    @pl.when(listed)
    def _():
        total = before[...] + split_dot(s_own[...], own[...]) + split_dot(s_oth[...], oth[...])
        if chained:
            earlier = jnp.concatenate([prev[j] for j in range(cols)], axis=1)
            total = total + split_dot(earlier, link[...])
        for j in range(cols):
            part[j] = -total[:, j * share : (j + 1) * share]
        quant, power = quantize(part[far])
        put(quant)
        spot = lax.broadcasted_iota(jnp.int32, powers.shape, 0) == step
        powers[...] = jnp.where(spot, jnp.broadcast_to(power, powers.shape), powers[...])

    @pl.when(jnp.logical_not(listed))
    def _():
        part[...] = jnp.zeros_like(part)
        put(jnp.zeros((TILE, share), i16))

    @pl.when(step == tiles - 1)
    def _():
        out_a[half:, :] = powers[...].astype(i16)
        out_b[out_b.shape[0] - PAD :, :] = powers[...].astype(i16)


def panel_specs(rows, depth, width, stream):
    block = rows // STREAMS
    by_lane = lambda i, m: (i, m[0] * STREAMS + stream)
    by_other = lambda i, m: (i, (1 - m[0]) * STREAMS + stream)
    whole = lambda i, m: (0, 0)
    return [
        pl.BlockSpec((TILE, block), by_lane),
        pl.BlockSpec((TILE, block), by_other),
        pl.BlockSpec((block, width), whole),
        pl.BlockSpec((block, width), whole),
    ]


def panel_first(meta, matrix, own, oth):
    rows, depth = matrix.shape
    width = own.shape[1]
    return pl.pallas_call(
        first_kernel,
        grid_spec=pltpu.PrefetchScalarGridSpec(
            num_scalar_prefetch=1,
            grid=(rows // TILE,),
            in_specs=panel_specs(rows, depth, width, 0),
            out_specs=pl.BlockSpec((TILE, width), lambda i, m: (i, 0)),
        ),
        out_shape=jax.ShapeDtypeStruct((rows, width), f32),
        compiler_params=pltpu.CompilerParams(vmem_limit_bytes=24 << 20),
        cost_estimate=pl.CostEstimate(
            flops=2 * rows * depth * width, bytes_accessed=2 * rows * depth, transcendentals=0
        ),
    )(meta, matrix, matrix, own, oth)


def panel_second(meta, matrix, own, oth, before, link, prev, cols):
    rows, depth = matrix.shape
    width = own.shape[1]
    share = width // cols
    half = rows // 2
    whole = lambda i, m: (0, 0)
    tile_of = pl.BlockSpec((cols, TILE, share), lambda i, m: (0, i, 0))
    in_specs = panel_specs(rows, depth, width, 1) + [pl.BlockSpec((TILE, width), lambda i, m: (i, 0))]
    operands = [matrix, matrix, own, oth, before]
    if link is not None:
        in_specs += [pl.BlockSpec((width, width), whole), tile_of]
        operands += [link, prev]
    message = jax.ShapeDtypeStruct((half + PAD, share), i16)
    return pl.pallas_call(
        functools.partial(second_kernel, cols, link is not None),
        grid_spec=pltpu.PrefetchScalarGridSpec(
            num_scalar_prefetch=1,
            grid=(rows // TILE,),
            in_specs=in_specs,
            out_specs=[tile_of] + [pl.BlockSpec((half + PAD, share), whole)] * 2,
            scratch_shapes=[pltpu.VMEM((PAD, share), jnp.int32)],
        ),
        out_shape=[jax.ShapeDtypeStruct((cols, rows, share), f32), message, message],
        compiler_params=pltpu.CompilerParams(vmem_limit_bytes=28 << 20),
        cost_estimate=pl.CostEstimate(
            flops=2 * rows * depth * width, bytes_accessed=2 * rows * depth, transcendentals=0
        ),
    )(meta, *operands)


def pass_kernel(meta, right, left, got_right, got_left, out_right, out_left):
    rows = right.shape[1]
    spot = lax.broadcasted_iota(jnp.int32, (PAD, right.shape[2]), 0)
    for mine, got, out, low in ((right, got_right, out_right, True), (left, got_left, out_left, False)):
        count = got.shape[0] - PAD
        begin = 0 if low else rows - count
        powers = jnp.zeros(spot.shape, jnp.int32)
        for tile in range(rows // TILE):
            at = tile * TILE
            total = mine[0, at : at + TILE, :]
            if begin <= at < begin + count:
                total = total + restore(got, at - begin, tile)
            quant, power = quantize(total)
            out[at : at + TILE, :] = quant
            powers = jnp.where(spot == tile, jnp.broadcast_to(power, spot.shape), powers)
        out[rows:, :] = powers.astype(i16)


def pass_on(meta, part, got_right, got_left, hop):
    cols, rows, share = part.shape
    everything = lambda i, m: (0, 0)
    message = jax.ShapeDtypeStruct((rows + PAD, share), i16)
    return pl.pallas_call(
        pass_kernel,
        grid_spec=pltpu.PrefetchScalarGridSpec(
            num_scalar_prefetch=1,
            grid=(1,),
            in_specs=[
                pl.BlockSpec((1, rows, share), lambda i, m: (lax.rem(m[1] + hop, cols), 0, 0)),
                pl.BlockSpec((1, rows, share), lambda i, m: (lax.rem(m[1] + cols - hop, cols), 0, 0)),
                pl.BlockSpec(got_right.shape, everything),
                pl.BlockSpec(got_left.shape, everything),
            ],
            out_specs=[pl.BlockSpec((rows + PAD, share), everything)] * 2,
        ),
        out_shape=[message, message],
        compiler_params=pltpu.CompilerParams(vmem_limit_bytes=20 << 20),
    )(meta, part, part, got_right, got_left)


def sum_kernel(tiles, count, meta, mine, got_right, got_left, *rest):
    factors = rest[:count]
    x_ref, sums = rest[-2:]
    step = pl.program_id(0)

    @pl.when(step == 0)
    def _():
        sums[...] = jnp.zeros_like(sums)

    for tile in range(tiles):

        @pl.when(step == tile)
        def _(tile=tile):
            total = mine[0]
            for got, low in ((got_right, True), (got_left, False)):
                rows = got.shape[0] - PAD
                begin = 0 if low else tiles * TILE - rows
                if begin <= tile * TILE < begin + rows:
                    total = total + restore(got, tile * TILE - begin, tile)
            x_ref[0] = total

    turned = x_ref[0].T
    width = factors[0].shape[2]
    for n, factor in enumerate(factors):
        sums[:, n * width : (n + 1) * width] += split_dot(turned, factor[0])


def sum_parts(meta, part, got_right, got_left, panels, k, carried):
    cols, rows, share = part.shape
    supernodes, _, width = panels.shape
    tiles = rows // TILE
    count = 1 if k + 1 == supernodes else 2
    everything = lambda i, m: (0, 0)
    in_specs = [
        pl.BlockSpec((1, TILE, share), lambda i, m: (m[1], i, 0)),
        pl.BlockSpec(got_right.shape, everything),
        pl.BlockSpec(got_left.shape, everything),
    ] + [pl.BlockSpec((1, TILE, width), lambda i, m, n=n: (k + n, i, 0)) for n in range(count)]
    operands = [part, got_right, got_left] + [panels] * count
    aliases = {}
    if carried is not None:
        in_specs.append(pl.BlockSpec(memory_space=pl.ANY))
        operands.append(carried)
        aliases = {len(operands): 0}
    return pl.pallas_call(
        functools.partial(sum_kernel, tiles, count),
        grid_spec=pltpu.PrefetchScalarGridSpec(
            num_scalar_prefetch=1,
            grid=(tiles,),
            in_specs=in_specs,
            out_specs=[
                pl.BlockSpec((1, TILE, share), lambda i, m: (k, i, 0)),
                pl.BlockSpec((share, count * width), everything),
            ],
        ),
        out_shape=[
            jax.ShapeDtypeStruct((supernodes, rows, share), f32),
            jax.ShapeDtypeStruct((share, count * width), f32),
        ],
        input_output_aliases=aliases,
        compiler_params=pltpu.CompilerParams(vmem_limit_bytes=20 << 20),
    )(meta, *operands)


def around(pieces, col_number):
    size = len(pieces)
    ring = jnp.stack(pieces[::-1] + pieces[:0:-1])
    return lax.dynamic_slice_in_dim(ring, size - 1 - col_number, size, 0)


def row_sum_half(value, lane, row_size):
    half = value.shape[0] // 2
    keep = lax.dynamic_slice_in_dim(value, lane * half, half, 0)
    give = lax.dynamic_slice_in_dim(value, (1 - lane) * half, half, 0)
    keep = keep + swap(give, 1, row_size)
    bit = 2
    while bit < row_size:
        keep = keep + swap(keep, bit, row_size)
        bit *= 2
    return keep


def both_halves(half, lane, row_size, axis):
    other = swap(half, 1, row_size)
    pick = lane == 0
    return jnp.concatenate(
        [jnp.where(pick, half, other), jnp.where(pick, other, half)], axis=axis
    )


def gather_chain(chunks, turn, order, row_size):
    size, supernodes = len(order), len(chunks)
    got = []
    for step in range(supernodes + size - 2):
        pairs = []
        for t in range(size - 1):
            if 0 <= step - t < supernodes:
                for c in range(size):
                    for i in range(LANES):
                        source = ((c ^ order[t]) * LANES + i) * size + c
                        target = ((c ^ order[t + 1]) * LANES + i) * size + c
                        pairs.append((source, target))
        if step == 0:
            value = chunks[0]
        elif step < supernodes:
            value = jnp.where(turn == 0, chunks[step], got[step - 1])
        else:
            value = got[step - 1]
        got.append(lax.ppermute(value, BOTH, pairs))
    found = []
    for k in range(supernodes):
        value = chunks[k]
        for t in range(1, size):
            value = jnp.where(turn == t, got[k + t - 1], value)
        found.append(value)
    return found


def local(inverse_block, tile_list, panels, links, diag_inverse):
    rows_here = inverse_block.shape[0]
    share = diag_inverse.shape[2]
    row_size, col_size = lax.axis_size("row"), lax.axis_size("col")
    row_number, col_number = lax.axis_index("row"), lax.axis_index("col")
    place, lane = row_number // LANES, row_number % LANES
    supernodes, _, width = panels.shape
    tiles_here = rows_here // TILE
    tiles = row_number * tiles_here + jnp.arange(tiles_here, dtype=jnp.int32)
    flags = jnp.any(tile_list[None, :] == tiles[:, None], axis=1)
    row_mask = jnp.broadcast_to(flags[:, None], (tiles_here, TILE)).reshape(-1, 1)
    meta = jnp.concatenate(
        [jnp.stack([lane, col_number]).astype(jnp.int32), flags.astype(jnp.int32)]
    )

    order = [t ^ (t >> 1) for t in range(col_size)]
    back = [order[-t] for t in range(col_size)]
    relative = place ^ col_number
    turn = sum(jnp.where(relative == order[t], t, 0) for t in range(col_size))
    turn_back = (col_size - turn) % col_size
    piece = rows_here // (2 * STREAMS)
    found = []
    for stream in range(STREAMS):
        ways = []
        for way, (path, at) in enumerate(((order, turn), (back, turn_back))):
            rows = slice((2 * stream + way) * piece, (2 * stream + way + 1) * piece)
            chunks = [
                jnp.where(row_mask[rows], panels[k, rows], jnp.zeros((), bf16))
                for k in range(supernodes)
            ]
            ways.append(gather_chain(chunks, at, path, row_size))
        found.append(ways)

    flat = links.reshape(-1, width)
    half = flat.shape[0] // 2
    my_links = lax.dynamic_slice_in_dim(flat, lane * half, half, 0)
    got = around([my_links] + [shift(my_links, s, col_size) for s in range(1, col_size)], col_number)
    link_full = both_halves(got, lane, row_size, 1)
    link_full = link_full.reshape(col_size, supernodes - 1, -1, width)
    link_full = link_full.transpose(1, 0, 2, 3).reshape(supernodes - 1, width, width)

    cross_parts, diag_parts = [], []
    part = carried = cross = stacked = full_turned = None
    for k in range(supernodes):
        last = k + 1 == supernodes
        own = [jnp.concatenate([found[s][0][k], found[s][1][k]], axis=0) for s in range(STREAMS)]
        oth = [swap(value, 1, row_size) for value in own]
        before = panel_first(meta, inverse_block, own[0], oth[0])
        link = None if k == 0 else link_full[k - 1]
        part, right, left = panel_second(
            meta, inverse_block, own[1], oth[1], before, link, part, col_size
        )
        for hop in range(col_size // 2 - 1, -1, -1):
            right, left = shift(right, 1, col_size), shift(left, -1, col_size)
            if hop > 0:
                right, left = pass_on(meta, part, right, left, hop)
        carried, sums = sum_parts(meta, part, right, left, panels, k, carried)

        summed = row_sum_half(sums, lane, row_size)
        mine = lax.dynamic_slice_in_dim(diag_inverse[k], lane * (share // 2), share // 2, 1).T
        turned = mine - summed[:, :width]
        if k > 0:
            link_wide = link.astype(f32)
            link_share = lax.dynamic_slice_in_dim(link_wide, col_number * share, share, 1)
            cross = -(stacked + turned_product(full_turned, link_share))
            cross_parts.append(cross)
            cross_half = lax.dynamic_slice_in_dim(cross, lane * (share // 2), share // 2, 1)
            turned = turned - turned_product(cross_half, link_wide)
        if last:
            diag_parts.append(both_halves(turned, lane, row_size, 0).T)
        else:
            arrived = []
            for s in range(col_size):
                at = (col_number + s) % col_size * share
                block = lax.dynamic_slice_in_dim(summed[:, width:], at, share, 1)
                message = jnp.concatenate([turned, block], axis=1)
                arrived.append(shift(message, s, col_size) if s else message)
            ordered = both_halves(around(arrived, col_number), lane, row_size, 1)
            full_turned = ordered[:, :, :width].reshape(width, width)
            stacked = ordered[:, :, width:].reshape(width, share)
            diag_parts.append(
                lax.dynamic_slice_in_dim(full_turned, col_number * share, share, 0).T
            )
    return carried, jnp.stack(cross_parts), jnp.stack(diag_parts)


def solution(mesh):
    in_specs = (
        P("row", "col"),
        P(),
        P(None, "row", None),
        P(None, "col", None),
        P(None, None, "col"),
    )
    out_specs = (P(None, "row", "col"), P(None, None, "col"), P(None, None, "col"))
    return jax.shard_map(local, mesh=mesh, in_specs=in_specs, out_specs=out_specs, check_vma=False)
```

```python
import functools

import jax
import jax.numpy as jnp
from jax import lax
from jax.experimental import pallas as pl
from jax.experimental.pallas import tpu as pltpu
from jax.sharding import PartitionSpec as P

TILE = 256
PAD = 16
LANES = 2
STREAMS = 2
FEED_COST = 10_000_000_000
HEAD = 4

precise = lax.Precision.HIGHEST
f32 = jnp.float32
bf16 = jnp.bfloat16
i16 = jnp.int16
BOTH = ("row", "col")


def product(left, right):
    return jnp.dot(left, right, precision=precise, preferred_element_type=f32)


def turned_product(left, right):
    return lax.dot_general(
        left, right, (((0,), (0,)), ((), ())), precision=precise, preferred_element_type=f32
    )


def split_dot(value, right):
    high = value.astype(bf16)
    low = (value - high.astype(f32)).astype(bf16)
    return jnp.dot(high, right, preferred_element_type=f32) + jnp.dot(
        low, right, preferred_element_type=f32
    )


def shift(value, by, size):
    return lax.ppermute(value, "col", [(z, (z + by) % size) for z in range(size)])


def swap(value, bit, size):
    return lax.ppermute(value, "row", [(r, r ^ bit) for r in range(size)])


def quantize(value):
    top = jnp.max(jnp.abs(value), axis=0, keepdims=True)
    power = jnp.clip(jnp.ceil(jnp.log2(jnp.maximum(top, 1e-30))), -100.0, 100.0)
    scaled = jnp.clip(jnp.round(value * jnp.exp2(15.0 - power)), -32767.0, 32767.0)
    return scaled.astype(jnp.int32).astype(i16), power.astype(jnp.int32)


def restore(ref, at, tile):
    count = ref.shape[0] - PAD
    powers = ref[count:, :].astype(jnp.int32).astype(f32)
    scale = jnp.exp2(powers[tile : tile + 1, :] - 15.0)
    return ref[at : at + TILE, :].astype(jnp.int32).astype(f32) * scale


def first_kernel(meta, s_own, s_oth, own, oth, total):
    @pl.when(meta[HEAD + pl.program_id(0)] > 0)
    def _():
        total[...] = split_dot(s_own[...], own[...]) + split_dot(s_oth[...], oth[...])


def second_kernel(cols, chained, meta, s_own, s_oth, own, oth, before, *rest):
    rest = list(rest)
    if chained:
        link, prev = rest[:2]
        rest = rest[2:]
    part, out_a, out_b, powers = rest
    step = pl.program_id(0)
    tiles = pl.num_programs(0)
    share = part.shape[2]
    half = out_a.shape[0] - PAD
    far = lax.rem(meta[1] + cols // 2, cols)

    @pl.when(step == 0)
    def _():
        powers[...] = jnp.zeros_like(powers)

    def put(quant):
        at = step * TILE

        @pl.when(at < half)
        def _():
            out_a[pl.ds(pl.multiple_of(at, TILE), TILE), :] = quant

        @pl.when(at >= half)
        def _():
            out_b[pl.ds(pl.multiple_of(at - half, TILE), TILE), :] = quant

    listed = meta[HEAD + step] > 0

    @pl.when(listed)
    def _():
        total = before[...] + split_dot(s_own[...], own[...]) + split_dot(s_oth[...], oth[...])
        if chained:
            earlier = jnp.concatenate([prev[j] for j in range(cols)], axis=1)
            total = total + split_dot(earlier, link[...])
        for j in range(cols):
            part[j] = -total[:, j * share : (j + 1) * share]
        quant, power = quantize(part[far])
        put(quant)
        spot = lax.broadcasted_iota(jnp.int32, powers.shape, 0) == step
        powers[...] = jnp.where(spot, jnp.broadcast_to(power, powers.shape), powers[...])

    @pl.when(jnp.logical_not(listed))
    def _():
        part[...] = jnp.zeros_like(part)
        put(jnp.zeros((TILE, share), i16))

    @pl.when(step == tiles - 1)
    def _():
        out_a[half:, :] = powers[...].astype(i16)
        out_b[out_b.shape[0] - PAD :, :] = powers[...].astype(i16)


def panel_specs(rows, depth, width, stream):
    block = rows // STREAMS
    by_lane = lambda i, m: (i, m[0] * STREAMS + stream)
    by_other = lambda i, m: (i, (1 - m[0]) * STREAMS + stream)
    whole = lambda i, m: (0, 0)
    return [
        pl.BlockSpec((TILE, block), by_lane),
        pl.BlockSpec((TILE, block), by_other),
        pl.BlockSpec((block, width), whole),
        pl.BlockSpec((block, width), whole),
    ]


def panel_first(meta, matrix, own, oth):
    rows, depth = matrix.shape
    width = own.shape[1]
    return pl.pallas_call(
        first_kernel,
        grid_spec=pltpu.PrefetchScalarGridSpec(
            num_scalar_prefetch=1,
            grid=(rows // TILE,),
            in_specs=panel_specs(rows, depth, width, 0),
            out_specs=pl.BlockSpec((TILE, width), lambda i, m: (i, 0)),
        ),
        out_shape=jax.ShapeDtypeStruct((rows, width), f32),
        compiler_params=pltpu.CompilerParams(vmem_limit_bytes=24 << 20),
        cost_estimate=pl.CostEstimate(
            flops=2 * rows * depth * width, bytes_accessed=2 * rows * depth, transcendentals=0
        ),
    )(meta, matrix, matrix, own, oth)


def panel_second(meta, matrix, own, oth, before, link, prev, cols):
    rows, depth = matrix.shape
    width = own.shape[1]
    share = width // cols
    half = rows // 2
    whole = lambda i, m: (0, 0)
    tile_of = pl.BlockSpec((cols, TILE, share), lambda i, m: (0, i, 0))
    in_specs = panel_specs(rows, depth, width, 1) + [pl.BlockSpec((TILE, width), lambda i, m: (i, 0))]
    operands = [matrix, matrix, own, oth, before]
    if link is not None:
        in_specs += [pl.BlockSpec((width, width), whole), tile_of]
        operands += [link, prev]
    message = jax.ShapeDtypeStruct((half + PAD, share), i16)
    return pl.pallas_call(
        functools.partial(second_kernel, cols, link is not None),
        grid_spec=pltpu.PrefetchScalarGridSpec(
            num_scalar_prefetch=1,
            grid=(rows // TILE,),
            in_specs=in_specs,
            out_specs=[tile_of] + [pl.BlockSpec((half + PAD, share), whole)] * 2,
            scratch_shapes=[pltpu.VMEM((PAD, share), jnp.int32)],
        ),
        out_shape=[jax.ShapeDtypeStruct((cols, rows, share), f32), message, message],
        compiler_params=pltpu.CompilerParams(vmem_limit_bytes=28 << 20),
        cost_estimate=pl.CostEstimate(
            flops=2 * rows * depth * width, bytes_accessed=2 * rows * depth, transcendentals=0
        ),
    )(meta, *operands)


def pass_kernel(meta, right, left, got_right, got_left, out_right, out_left):
    rows = right.shape[1]
    spot = lax.broadcasted_iota(jnp.int32, (PAD, right.shape[2]), 0)
    for mine, got, out, low in ((right, got_right, out_right, True), (left, got_left, out_left, False)):
        count = got.shape[0] - PAD
        begin = 0 if low else rows - count
        powers = jnp.zeros(spot.shape, jnp.int32)
        for tile in range(rows // TILE):
            at = tile * TILE
            total = mine[0, at : at + TILE, :]
            if begin <= at < begin + count:
                total = total + restore(got, at - begin, tile)
            quant, power = quantize(total)
            out[at : at + TILE, :] = quant
            powers = jnp.where(spot == tile, jnp.broadcast_to(power, spot.shape), powers)
        out[rows:, :] = powers.astype(i16)


def pass_on(meta, part, got_right, got_left, hop):
    cols, rows, share = part.shape
    everything = lambda i, m: (0, 0)
    message = jax.ShapeDtypeStruct((rows + PAD, share), i16)
    return pl.pallas_call(
        pass_kernel,
        grid_spec=pltpu.PrefetchScalarGridSpec(
            num_scalar_prefetch=1,
            grid=(1,),
            in_specs=[
                pl.BlockSpec((1, rows, share), lambda i, m: (lax.rem(m[1] + hop, cols), 0, 0)),
                pl.BlockSpec((1, rows, share), lambda i, m: (lax.rem(m[1] + cols - hop, cols), 0, 0)),
                pl.BlockSpec(got_right.shape, everything),
                pl.BlockSpec(got_left.shape, everything),
            ],
            out_specs=[pl.BlockSpec((rows + PAD, share), everything)] * 2,
        ),
        out_shape=[message, message],
        compiler_params=pltpu.CompilerParams(vmem_limit_bytes=20 << 20),
    )(meta, part, part, got_right, got_left)


def sum_kernel(tiles, count, meta, mine, got_right, got_left, *rest):
    factors = rest[:count]
    x_ref, sums = rest[-2:]
    step = pl.program_id(0)

    @pl.when(step == 0)
    def _():
        sums[...] = jnp.zeros_like(sums)

    for tile in range(tiles):

        @pl.when(step == tile)
        def _(tile=tile):
            total = mine[0]
            for got, low in ((got_right, True), (got_left, False)):
                rows = got.shape[0] - PAD
                begin = 0 if low else tiles * TILE - rows
                if begin <= tile * TILE < begin + rows:
                    total = total + restore(got, tile * TILE - begin, tile)
            x_ref[0] = total

    turned = x_ref[0].T
    width = factors[0].shape[2]
    for n, factor in enumerate(factors):
        sums[:, n * width : (n + 1) * width] += split_dot(turned, factor[0])


def sum_parts(meta, part, got_right, got_left, panels, k, carried):
    cols, rows, share = part.shape
    supernodes, _, width = panels.shape
    tiles = rows // TILE
    count = 1 if k + 1 == supernodes else 2
    everything = lambda i, m: (0, 0)
    in_specs = [
        pl.BlockSpec((1, TILE, share), lambda i, m: (m[1], i, 0)),
        pl.BlockSpec(got_right.shape, everything),
        pl.BlockSpec(got_left.shape, everything),
    ] + [pl.BlockSpec((1, TILE, width), lambda i, m, n=n: (k + n, i, 0)) for n in range(count)]
    operands = [part, got_right, got_left] + [panels] * count
    aliases = {}
    if carried is not None:
        in_specs.append(pl.BlockSpec(memory_space=pl.ANY))
        operands.append(carried)
        aliases = {len(operands): 0}
    return pl.pallas_call(
        functools.partial(sum_kernel, tiles, count),
        grid_spec=pltpu.PrefetchScalarGridSpec(
            num_scalar_prefetch=1,
            grid=(tiles,),
            in_specs=in_specs,
            out_specs=[
                pl.BlockSpec((1, TILE, share), lambda i, m: (k, i, 0)),
                pl.BlockSpec((share, count * width), everything),
            ],
        ),
        out_shape=[
            jax.ShapeDtypeStruct((supernodes, rows, share), f32),
            jax.ShapeDtypeStruct((share, count * width), f32),
        ],
        input_output_aliases=aliases,
        compiler_params=pltpu.CompilerParams(vmem_limit_bytes=20 << 20),
    )(meta, *operands)


def around(pieces, col_number):
    size = len(pieces)
    ring = jnp.stack(pieces[::-1] + pieces[:0:-1])
    return lax.dynamic_slice_in_dim(ring, size - 1 - col_number, size, 0)


def row_sum_half(value, lane, row_size):
    half = value.shape[0] // 2
    keep = lax.dynamic_slice_in_dim(value, lane * half, half, 0)
    give = lax.dynamic_slice_in_dim(value, (1 - lane) * half, half, 0)
    keep = keep + swap(give, 1, row_size)
    bit = 2
    while bit < row_size:
        keep = keep + swap(keep, bit, row_size)
        bit *= 2
    return keep


def both_halves(half, lane, row_size, axis):
    other = swap(half, 1, row_size)
    pick = lane == 0
    return jnp.concatenate(
        [jnp.where(pick, half, other), jnp.where(pick, other, half)], axis=axis
    )


def after(value, *others):
    return lax.optimization_barrier((value, *others))[0]


def own_blocks(meta, row, rows):
    block = min(rows, TILE)
    return [(at, block, meta[HEAD + (row + at) // TILE]) for at in range(0, rows, block)]


def feed_kernel(spots, meta, *refs):
    ways = len(spots)
    own, outs = refs[:ways], refs[-ways:]
    arrived = refs[ways:-ways]
    for way, row in enumerate(spots):
        out = outs[way]

        def fill(way=way, row=row, out=out):
            for at, block, flag in own_blocks(meta, row, out.shape[0]):
                value = own[way][0, at : at + block, :]
                out[at : at + block, :] = jnp.where(flag > 0, value, jnp.zeros_like(value))

        if not arrived:
            fill()
        else:
            first = meta[2 + way] == 0
            pl.when(first)(fill)

            @pl.when(jnp.logical_not(first))
            def _(way=way, out=out):
                out[...] = arrived[way][...]


def feed(meta, panels, k, stream, arrived):
    _, rows, width = panels.shape
    ways = 2
    piece = rows // (ways * STREAMS)
    block = pl.BlockSpec((piece, width), lambda i, m: (0, 0))
    return pl.pallas_call(
        functools.partial(feed_kernel, [(stream * ways + way) * piece for way in range(ways)]),
        grid_spec=pltpu.PrefetchScalarGridSpec(
            num_scalar_prefetch=1,
            grid=(1,),
            in_specs=[
                pl.BlockSpec((1, piece, width), lambda i, m, w=w: (k, stream * ways + w, 0))
                for w in range(ways)
            ]
            + [block] * len(arrived),
            out_specs=[block] * ways,
        ),
        out_shape=[jax.ShapeDtypeStruct((piece, width), bf16)] * ways,
        cost_estimate=pl.CostEstimate(flops=FEED_COST, bytes_accessed=0, transcendentals=0),
    )(meta, *[panels] * ways, *arrived)


def pick_kernel(k, spots, meta, panels, *refs):
    ways = len(spots)
    zeros, sems = refs[-2:]
    out = refs[-3]
    turns = len(refs[:-3]) // ways
    piece = out.shape[0] // ways
    zeros[...] = jnp.zeros_like(zeros)

    def each(act):
        for way, row in enumerate(spots):
            base = way * piece
            turn = meta[2 + way]
            for t in range(turns):

                @pl.when(turn == t + 1)
                def _(way=way, t=t, base=base):
                    target = out.at[pl.ds(base, piece)]
                    act(pltpu.make_async_copy(refs[way * turns + t], target, sems.at[way, 0]))

            for n, (at, block, flag) in enumerate(own_blocks(meta, row, piece)):
                target = out.at[pl.ds(base + at, block)]

                @pl.when((turn == 0) & (flag > 0))
                def _(way=way, n=n, row=row, at=at, block=block, target=target):
                    source = panels.at[k, pl.ds(row + at, block)]
                    act(pltpu.make_async_copy(source, target, sems.at[way, n]))

                @pl.when((turn == 0) & (flag == 0))
                def _(way=way, n=n, target=target):
                    act(pltpu.make_async_copy(zeros, target, sems.at[way, n]))

    each(lambda copy: copy.start())
    each(lambda copy: copy.wait())


def pick(meta, panels, k, stream, received):
    _, rows, width = panels.shape
    ways = len(received)
    piece = rows // (ways * STREAMS)
    block = min(piece, TILE)
    operands = [panels] + [value for way in received for value in way]
    return pl.pallas_call(
        functools.partial(pick_kernel, k, [(stream * ways + way) * piece for way in range(ways)]),
        grid_spec=pltpu.PrefetchScalarGridSpec(
            num_scalar_prefetch=1,
            grid=(1,),
            in_specs=[pl.BlockSpec(memory_space=pl.ANY)] * len(operands),
            out_specs=pl.BlockSpec(memory_space=pl.ANY),
            scratch_shapes=[
                pltpu.VMEM((block, width), bf16),
                pltpu.SemaphoreType.DMA((ways, piece // block)),
            ],
        ),
        out_shape=jax.ShapeDtypeStruct((ways * piece, width), bf16),
    )(meta, *operands)


def send_on(values, orders, step, supernodes):
    size = len(orders[0])
    got = []
    for value, order in zip(values, orders):
        pairs = []
        for t in range(size - 1):
            if 0 <= step - t < supernodes:
                for c in range(size):
                    for i in range(LANES):
                        source = ((c ^ order[t]) * LANES + i) * size + c
                        target = ((c ^ order[t + 1]) * LANES + i) * size + c
                        pairs.append((source, target))
        got.append(lax.ppermute(value, BOTH, pairs))
    return got


def local(inverse_block, tile_list, panels, links, diag_inverse):
    rows_here = inverse_block.shape[0]
    share = diag_inverse.shape[2]
    row_size, col_size = lax.axis_size("row"), lax.axis_size("col")
    row_number, col_number = lax.axis_index("row"), lax.axis_index("col")
    place, lane = row_number // LANES, row_number % LANES
    supernodes, _, width = panels.shape
    tiles_here = rows_here // TILE
    tiles = row_number * tiles_here + jnp.arange(tiles_here, dtype=jnp.int32)
    flags = jnp.any(tile_list[None, :] == tiles[:, None], axis=1)

    order = [t ^ (t >> 1) for t in range(col_size)]
    back = [order[-t] for t in range(col_size)]
    orders = (order, back)
    relative = place ^ col_number
    turn = sum(jnp.where(relative == order[t], t, 0) for t in range(col_size))
    meta = jnp.concatenate(
        [
            jnp.stack([lane, col_number, turn, (col_size - turn) % col_size]).astype(jnp.int32),
            flags.astype(jnp.int32),
        ]
    )

    flat = links.reshape(-1, width)
    half = flat.shape[0] // 2
    my_links = lax.dynamic_slice_in_dim(flat, lane * half, half, 0)
    got = around([my_links] + [shift(my_links, s, col_size) for s in range(1, col_size)], col_number)
    link_full = both_halves(got, lane, row_size, 1)
    link_full = link_full.reshape(col_size, supernodes - 1, -1, width)
    link_full = link_full.transpose(1, 0, 2, 3).reshape(supernodes - 1, width, width)

    cross_parts, diag_parts = [], []
    carried = cross = stacked = full_turned = None
    events = []
    steps = supernodes + col_size - 2
    parts = []
    befores = []
    done = 0

    def arrive(n):
        nonlocal done
        while done < 2 * supernodes and 2 * (done // 2 + col_size - 2) + done % 2 <= n:
            k, stream = done // 2, done % 2
            received = [
                [events[2 * (k + t - 1) + stream][way] for t in range(1, col_size)]
                for way in range(2)
            ]
            own = pick(meta, panels, k, stream, received)
            oth = swap(own, 1, row_size)
            link = None if k == 0 else link_full[k - 1]
            if stream == 0:
                if k > 0:
                    own = after(own, parts[-1][0])
                befores.append(panel_first(meta, inverse_block, own, oth))
            else:
                parts.append(
                    panel_second(
                        meta, inverse_block, own, oth, befores[-1], link,
                        parts[-1][0] if k > 0 else None, col_size,
                    )
                )
            done += 1

    for step in range(steps):
        for stream in range(STREAMS):
            arrived = events[-STREAMS] if step > 0 else []
            if step < supernodes:
                values = feed(meta, panels, step, stream, arrived)
            else:
                values = arrived
            tie = events[-STREAMS - 1] if len(events) > STREAMS else []
            if len(events) == 2 * col_size - 1 and befores:
                tie = tie + befores[:1]
            elif len(events) == 2 * col_size + 1 and parts:
                tie = tie + [parts[0][0]]
            values = lax.optimization_barrier((*values, *tie))[: len(orders)]
            events.append(send_on(values, orders, step, supernodes))
            arrive(len(events) - 1)
    hops = []
    for part, right, left in parts:
        stages = []
        for hop in range(col_size // 2 - 1, -1, -1):
            right, left = shift(right, 1, col_size), shift(left, -1, col_size)
            stages.append((right, left))
            if hop > 0:
                right, left = pass_on(meta, part, right, left, hop)
                stages.append((right, left))
        hops.append(stages)
    gates = [[befores[-1]]] + [hops[-1][0]] * (supernodes - 2) + [()]
    for k in range(supernodes):
        last = k + 1 == supernodes
        link = None if k == 0 else link_full[k - 1]
        part = parts[k][0]
        right, left = hops[k][-1]
        carried, sums = sum_parts(meta, part, right, left, panels, k, carried)
        sums = after(sums, *gates[k])

        summed = row_sum_half(sums, lane, row_size)
        mine = lax.dynamic_slice_in_dim(diag_inverse[k], lane * (share // 2), share // 2, 1).T
        turned = mine - summed[:, :width]
        if k > 0:
            link_wide = link.astype(f32)
            link_share = lax.dynamic_slice_in_dim(link_wide, col_number * share, share, 1)
            cross = -(stacked + turned_product(full_turned, link_share))
            cross_parts.append(cross)
            cross_half = lax.dynamic_slice_in_dim(cross, lane * (share // 2), share // 2, 1)
            turned = turned - turned_product(cross_half, link_wide)
        if last:
            diag_parts.append(both_halves(turned, lane, row_size, 0).T)
        else:
            arrived = []
            for s in range(col_size):
                at = (col_number + s) % col_size * share
                block = lax.dynamic_slice_in_dim(summed[:, width:], at, share, 1)
                message = jnp.concatenate([turned, block], axis=1)
                message = after(message, *hops[-1][min(1, len(hops[-1]) - 1)])
                arrived.append(shift(message, s, col_size) if s else message)
            ordered = both_halves(around(arrived, col_number), lane, row_size, 1)
            full_turned = ordered[:, :, :width].reshape(width, width)
            stacked = ordered[:, :, width:].reshape(width, share)
            diag_parts.append(
                lax.dynamic_slice_in_dim(full_turned, col_number * share, share, 0).T
            )
    return carried, jnp.stack(cross_parts), jnp.stack(diag_parts)


def solution(mesh):
    in_specs = (
        P("row", "col"),
        P(),
        P(None, "row", None),
        P(None, "col", None),
        P(None, None, "col"),
    )
    out_specs = (P(None, "row", "col"), P(None, None, "col"), P(None, None, "col"))
    return jax.shard_map(local, mesh=mesh, in_specs=in_specs, out_specs=out_specs, check_vma=False)
```

```python
import functools

import jax
import jax.numpy as jnp
from jax import lax
from jax.experimental import pallas as pl
from jax.experimental.pallas import tpu as pltpu
from jax.sharding import PartitionSpec as P

TILE = 256
PAD = 16
LANES = 2
STREAMS = 2
FEED_COST = 10_000_000_000
VMEM = 24 << 20
HEAD = 4

precise = lax.Precision.HIGHEST
f32 = jnp.float32
bf16 = jnp.bfloat16
i16 = jnp.int16
BOTH = ("row", "col")


def product(left, right):
    return jnp.dot(left, right, precision=precise, preferred_element_type=f32)


def turned_product(left, right):
    return lax.dot_general(
        left, right, (((0,), (0,)), ((), ())), precision=precise, preferred_element_type=f32
    )


def split_dot(value, right):
    high = value.astype(bf16)
    low = (value - high.astype(f32)).astype(bf16)
    return jnp.dot(high, right, preferred_element_type=f32) + jnp.dot(
        low, right, preferred_element_type=f32
    )


def shift(value, by, size):
    return lax.ppermute(value, "col", [(z, (z + by) % size) for z in range(size)])


def swap(value, bit, size):
    return lax.ppermute(value, "row", [(r, r ^ bit) for r in range(size)])


def quantize(value):
    top = jnp.max(jnp.abs(value), axis=0, keepdims=True)
    power = jnp.clip(jnp.ceil(jnp.log2(jnp.maximum(top, 1e-30))), -100.0, 100.0)
    scaled = jnp.clip(jnp.round(value * jnp.exp2(15.0 - power)), -32767.0, 32767.0)
    return scaled.astype(jnp.int32).astype(i16), power.astype(jnp.int32)


def restore(ref, at, tile):
    count = ref.shape[0] - PAD
    powers = ref[count:, :].astype(jnp.int32).astype(f32)
    scale = jnp.exp2(powers[tile : tile + 1, :] - 15.0)
    return ref[at : at + TILE, :].astype(jnp.int32).astype(f32) * scale


def first_kernel(meta, s_own, s_oth, own, oth, total):
    @pl.when(meta[HEAD + pl.program_id(0)] > 0)
    def _():
        total[...] = split_dot(s_own[...], own[...]) + split_dot(s_oth[...], oth[...])


def second_kernel(cols, chained, meta, s_own, s_oth, own, oth, before, *rest):
    rest = list(rest)
    if chained:
        link, prev = rest[:2]
        rest = rest[2:]
    part, out_a, out_b, powers = rest
    step = pl.program_id(0)
    tiles = pl.num_programs(0)
    share = part.shape[2]
    half = out_a.shape[0] - PAD
    far = lax.rem(meta[1] + cols // 2, cols)

    @pl.when(step == 0)
    def _():
        powers[...] = jnp.zeros_like(powers)

    def put(quant):
        at = step * TILE

        @pl.when(at < half)
        def _():
            out_a[pl.ds(pl.multiple_of(at, TILE), TILE), :] = quant

        @pl.when(at >= half)
        def _():
            out_b[pl.ds(pl.multiple_of(at - half, TILE), TILE), :] = quant

    listed = meta[HEAD + step] > 0

    @pl.when(listed)
    def _():
        total = before[...] + split_dot(s_own[...], own[...]) + split_dot(s_oth[...], oth[...])
        if chained:
            earlier = jnp.concatenate([prev[j] for j in range(cols)], axis=1)
            total = total + split_dot(earlier, link[...])
        for j in range(cols):
            part[j] = -total[:, j * share : (j + 1) * share]
        quant, power = quantize(part[far])
        put(quant)
        spot = lax.broadcasted_iota(jnp.int32, powers.shape, 0) == step
        powers[...] = jnp.where(spot, jnp.broadcast_to(power, powers.shape), powers[...])

    @pl.when(jnp.logical_not(listed))
    def _():
        part[...] = jnp.zeros_like(part)
        put(jnp.zeros((TILE, share), i16))

    @pl.when(step == tiles - 1)
    def _():
        out_a[half:, :] = powers[...].astype(i16)
        out_b[out_b.shape[0] - PAD :, :] = powers[...].astype(i16)


def panel_specs(rows, depth, width, stream):
    block = rows // STREAMS
    by_lane = lambda i, m: (i, m[0] * STREAMS + stream)
    by_other = lambda i, m: (i, (1 - m[0]) * STREAMS + stream)
    whole = lambda i, m: (0, 0)
    return [
        pl.BlockSpec((TILE, block), by_lane),
        pl.BlockSpec((TILE, block), by_other),
        pl.BlockSpec((block, width), whole),
        pl.BlockSpec((block, width), whole),
    ]


def panel_first(meta, matrix, own, oth):
    rows, depth = matrix.shape
    width = own.shape[1]
    return pl.pallas_call(
        first_kernel,
        grid_spec=pltpu.PrefetchScalarGridSpec(
            num_scalar_prefetch=1,
            grid=(rows // TILE,),
            in_specs=panel_specs(rows, depth, width, 0),
            out_specs=pl.BlockSpec((TILE, width), lambda i, m: (i, 0)),
        ),
        out_shape=jax.ShapeDtypeStruct((rows, width), f32),
        compiler_params=pltpu.CompilerParams(vmem_limit_bytes=VMEM),
        cost_estimate=pl.CostEstimate(
            flops=2 * rows * depth * width, bytes_accessed=2 * rows * depth, transcendentals=0
        ),
    )(meta, matrix, matrix, own, oth)


def panel_second(meta, matrix, own, oth, before, link, prev, cols):
    rows, depth = matrix.shape
    width = own.shape[1]
    share = width // cols
    half = rows // 2
    whole = lambda i, m: (0, 0)
    tile_of = pl.BlockSpec((cols, TILE, share), lambda i, m: (0, i, 0))
    in_specs = panel_specs(rows, depth, width, 1) + [pl.BlockSpec((TILE, width), lambda i, m: (i, 0))]
    operands = [matrix, matrix, own, oth, before]
    if link is not None:
        in_specs += [pl.BlockSpec((width, width), whole), tile_of]
        operands += [link, prev]
    message = jax.ShapeDtypeStruct((half + PAD, share), i16)
    return pl.pallas_call(
        functools.partial(second_kernel, cols, link is not None),
        grid_spec=pltpu.PrefetchScalarGridSpec(
            num_scalar_prefetch=1,
            grid=(rows // TILE,),
            in_specs=in_specs,
            out_specs=[tile_of] + [pl.BlockSpec((half + PAD, share), whole)] * 2,
            scratch_shapes=[pltpu.VMEM((PAD, share), jnp.int32)],
        ),
        out_shape=[jax.ShapeDtypeStruct((cols, rows, share), f32), message, message],
        compiler_params=pltpu.CompilerParams(vmem_limit_bytes=VMEM),
        cost_estimate=pl.CostEstimate(
            flops=2 * rows * depth * width, bytes_accessed=2 * rows * depth, transcendentals=0
        ),
    )(meta, *operands)


def pass_kernel(meta, right, left, got_right, got_left, out_right, out_left):
    rows = right.shape[1]
    spot = lax.broadcasted_iota(jnp.int32, (PAD, right.shape[2]), 0)
    for mine, got, out, low in ((right, got_right, out_right, True), (left, got_left, out_left, False)):
        count = got.shape[0] - PAD
        begin = 0 if low else rows - count
        powers = jnp.zeros(spot.shape, jnp.int32)
        for tile in range(rows // TILE):
            at = tile * TILE
            total = mine[0, at : at + TILE, :]
            if begin <= at < begin + count:
                total = total + restore(got, at - begin, tile)
            quant, power = quantize(total)
            out[at : at + TILE, :] = quant
            powers = jnp.where(spot == tile, jnp.broadcast_to(power, spot.shape), powers)
        out[rows:, :] = powers.astype(i16)


def pass_on(meta, part, got_right, got_left, hop):
    cols, rows, share = part.shape
    everything = lambda i, m: (0, 0)
    message = jax.ShapeDtypeStruct((rows + PAD, share), i16)
    return pl.pallas_call(
        pass_kernel,
        grid_spec=pltpu.PrefetchScalarGridSpec(
            num_scalar_prefetch=1,
            grid=(1,),
            in_specs=[
                pl.BlockSpec((1, rows, share), lambda i, m: (lax.rem(m[1] + hop, cols), 0, 0)),
                pl.BlockSpec((1, rows, share), lambda i, m: (lax.rem(m[1] + cols - hop, cols), 0, 0)),
                pl.BlockSpec(got_right.shape, everything),
                pl.BlockSpec(got_left.shape, everything),
            ],
            out_specs=[pl.BlockSpec((rows + PAD, share), everything)] * 2,
        ),
        out_shape=[message, message],
        compiler_params=pltpu.CompilerParams(vmem_limit_bytes=VMEM),
    )(meta, part, part, got_right, got_left)


def sum_kernel(tiles, count, meta, mine, got_right, got_left, *rest):
    factors = rest[:count]
    x_ref, sums = rest[-2:]
    step = pl.program_id(0)

    @pl.when(step == 0)
    def _():
        sums[...] = jnp.zeros_like(sums)

    for tile in range(tiles):

        @pl.when(step == tile)
        def _(tile=tile):
            total = mine[0]
            for got, low in ((got_right, True), (got_left, False)):
                rows = got.shape[0] - PAD
                begin = 0 if low else tiles * TILE - rows
                if begin <= tile * TILE < begin + rows:
                    total = total + restore(got, tile * TILE - begin, tile)
            x_ref[0] = total

    turned = x_ref[0].T
    width = factors[0].shape[2]
    for n, factor in enumerate(factors):
        sums[:, n * width : (n + 1) * width] += split_dot(turned, factor[0])


def sum_parts(meta, part, got_right, got_left, panels, k, carried):
    cols, rows, share = part.shape
    supernodes, _, width = panels.shape
    tiles = rows // TILE
    count = 1 if k + 1 == supernodes else 2
    everything = lambda i, m: (0, 0)
    in_specs = [
        pl.BlockSpec((1, TILE, share), lambda i, m: (m[1], i, 0)),
        pl.BlockSpec(got_right.shape, everything),
        pl.BlockSpec(got_left.shape, everything),
    ] + [pl.BlockSpec((1, TILE, width), lambda i, m, n=n: (k + n, i, 0)) for n in range(count)]
    operands = [part, got_right, got_left] + [panels] * count
    aliases = {}
    if carried is not None:
        in_specs.append(pl.BlockSpec(memory_space=pl.ANY))
        operands.append(carried)
        aliases = {len(operands): 0}
    return pl.pallas_call(
        functools.partial(sum_kernel, tiles, count),
        grid_spec=pltpu.PrefetchScalarGridSpec(
            num_scalar_prefetch=1,
            grid=(tiles,),
            in_specs=in_specs,
            out_specs=[
                pl.BlockSpec((1, TILE, share), lambda i, m: (k, i, 0)),
                pl.BlockSpec((share, count * width), everything),
            ],
        ),
        out_shape=[
            jax.ShapeDtypeStruct((supernodes, rows, share), f32),
            jax.ShapeDtypeStruct((share, count * width), f32),
        ],
        input_output_aliases=aliases,
        compiler_params=pltpu.CompilerParams(vmem_limit_bytes=VMEM),
    )(meta, *operands)


def around(pieces, col_number):
    size = len(pieces)
    ring = jnp.stack(pieces[::-1] + pieces[:0:-1])
    return lax.dynamic_slice_in_dim(ring, size - 1 - col_number, size, 0)


def row_sum_half(value, lane, row_size, gates=()):
    half = value.shape[0] // 2
    keep = lax.dynamic_slice_in_dim(value, lane * half, half, 0)
    give = lax.dynamic_slice_in_dim(value, (1 - lane) * half, half, 0)
    stages = [keep + swap(give, 1, row_size)]
    bit = 2
    while bit < row_size:
        value = stages[-1]
        if len(stages) <= len(gates):
            value = after(value, *gates[len(stages) - 1])
        stages.append(value + swap(value, bit, row_size))
        bit *= 2
    return stages


def both_halves(half, lane, row_size, axis):
    other = swap(half, 1, row_size)
    pick = lane == 0
    return jnp.concatenate(
        [jnp.where(pick, half, other), jnp.where(pick, other, half)], axis=axis
    )


def after(value, *others):
    return lax.optimization_barrier((value, *others))[0]


def own_blocks(meta, row, rows):
    block = min(rows, TILE)
    return [(at, block, meta[HEAD + (row + at) // TILE]) for at in range(0, rows, block)]


def feed_kernel(spots, meta, *refs):
    ways = len(spots)
    own, outs = refs[:ways], refs[-ways:]
    arrived = refs[ways:-ways]
    for way, row in enumerate(spots):
        out = outs[way]

        def fill(way=way, row=row, out=out):
            for at, block, flag in own_blocks(meta, row, out.shape[0]):
                value = own[way][0, at : at + block, :]
                out[at : at + block, :] = jnp.where(flag > 0, value, jnp.zeros_like(value))

        if not arrived:
            fill()
        else:
            first = meta[2 + way] == 0
            pl.when(first)(fill)

            @pl.when(jnp.logical_not(first))
            def _(way=way, out=out):
                out[...] = arrived[way][...]


def feed(meta, panels, k, stream, arrived):
    _, rows, width = panels.shape
    ways = 2
    piece = rows // (ways * STREAMS)
    block = pl.BlockSpec((piece, width), lambda i, m: (0, 0))
    return pl.pallas_call(
        functools.partial(feed_kernel, [(stream * ways + way) * piece for way in range(ways)]),
        grid_spec=pltpu.PrefetchScalarGridSpec(
            num_scalar_prefetch=1,
            grid=(1,),
            in_specs=[
                pl.BlockSpec((1, piece, width), lambda i, m, w=w: (k, stream * ways + w, 0))
                for w in range(ways)
            ]
            + [block] * len(arrived),
            out_specs=[block] * ways,
        ),
        out_shape=[jax.ShapeDtypeStruct((piece, width), bf16)] * ways,
        compiler_params=pltpu.CompilerParams(vmem_limit_bytes=VMEM),
        cost_estimate=pl.CostEstimate(flops=FEED_COST, bytes_accessed=0, transcendentals=0),
    )(meta, *[panels] * ways, *arrived)


def pick_kernel(k, spots, meta, panels, *refs):
    ways = len(spots)
    out, sems = refs[-2:]
    turns = len(refs[:-2]) // ways
    piece = out.shape[0] // ways

    def each(act):
        for way, row in enumerate(spots):
            base = way * piece
            turn = meta[2 + way]
            for t in range(turns):

                @pl.when(turn == t + 1)
                def _(way=way, t=t, base=base):
                    target = out.at[pl.ds(base, piece)]
                    act(pltpu.make_async_copy(refs[way * turns + t], target, sems.at[way, 0]))

            for n, (at, block, flag) in enumerate(own_blocks(meta, row, piece)):
                target = out.at[pl.ds(base + at, block)]

                @pl.when((turn == 0) & (flag > 0))
                def _(way=way, n=n, row=row, at=at, block=block, target=target):
                    source = panels.at[k, pl.ds(row + at, block)]
                    act(pltpu.make_async_copy(source, target, sems.at[way, n]))


    each(lambda copy: copy.start())
    for way, row in enumerate(spots):
        for at, block, flag in own_blocks(meta, row, piece):

            @pl.when((meta[2 + way] == 0) & (flag == 0))
            def _(at=way * piece + at, block=block):
                out[at : at + block, :] = jnp.zeros((block, out.shape[1]), out.dtype)

    each(lambda copy: copy.wait())


def pick(meta, panels, k, stream, received):
    _, rows, width = panels.shape
    ways = len(received)
    piece = rows // (ways * STREAMS)
    block = min(piece, TILE)
    operands = [panels] + [value for way in received for value in way]
    return pl.pallas_call(
        functools.partial(pick_kernel, k, [(stream * ways + way) * piece for way in range(ways)]),
        grid_spec=pltpu.PrefetchScalarGridSpec(
            num_scalar_prefetch=1,
            grid=(1,),
            in_specs=[pl.BlockSpec(memory_space=pltpu.HBM)] * len(operands),
            out_specs=pl.BlockSpec((ways * piece, width), lambda i, m: (0, 0)),
            scratch_shapes=[pltpu.SemaphoreType.DMA((ways, piece // block))],
        ),
        out_shape=jax.ShapeDtypeStruct((ways * piece, width), bf16),
        compiler_params=pltpu.CompilerParams(vmem_limit_bytes=VMEM),
    )(meta, *operands)


def send_on(values, orders, step, supernodes):
    size = len(orders[0])
    got = []
    for value, order in zip(values, orders):
        pairs = []
        for t in range(size - 1):
            if 0 <= step - t < supernodes:
                for c in range(size):
                    for i in range(LANES):
                        source = ((c ^ order[t]) * LANES + i) * size + c
                        target = ((c ^ order[t + 1]) * LANES + i) * size + c
                        pairs.append((source, target))
        got.append(lax.ppermute(value, BOTH, pairs))
    return got


def local(inverse_block, tile_list, panels, links, diag_inverse):
    rows_here = inverse_block.shape[0]
    share = diag_inverse.shape[2]
    row_size, col_size = lax.axis_size("row"), lax.axis_size("col")
    row_number, col_number = lax.axis_index("row"), lax.axis_index("col")
    place, lane = row_number // LANES, row_number % LANES
    supernodes, _, width = panels.shape
    tiles_here = rows_here // TILE
    tiles = row_number * tiles_here + jnp.arange(tiles_here, dtype=jnp.int32)
    flags = jnp.any(tile_list[None, :] == tiles[:, None], axis=1)

    order = [t ^ (t >> 1) for t in range(col_size)]
    back = [order[-t] for t in range(col_size)]
    orders = (order, back)
    relative = place ^ col_number
    turn = sum(jnp.where(relative == order[t], t, 0) for t in range(col_size))
    meta = jnp.concatenate(
        [
            jnp.stack([lane, col_number, turn, (col_size - turn) % col_size]).astype(jnp.int32),
            flags.astype(jnp.int32),
        ]
    )

    cross_parts, diag_parts = [], []
    carried = cross = stacked = full_turned = None
    link_full = None
    events = []
    steps = supernodes + col_size - 2
    parts, products, hops, sums, summed = [], [], [], [], []
    done = 0

    picked = []

    def finish(k, ties=(), gates=()):
        nonlocal carried
        right, left = hops[k][-1]
        if ties:
            right = after(right, *ties)
        carried, total = sum_parts(meta, parts[k], right, left, panels, k, carried)
        sums.append(total)
        summed.append(row_sum_half(total, lane, row_size, gates))

    def scatter(k):
        right, left = hops[k][-1]
        for hop in range(col_size // 2 - 1, 0, -1):
            right = after(right, products[-1])
            right, left = pass_on(meta, parts[k], right, left, hop)
            hops[k].append((right, left))
            right, left = shift(right, 1, col_size), shift(left, -1, col_size)
            hops[k].append((right, left))

    def pick_now(q):
        k, stream = q // 2, q % 2
        flat = [
            events[2 * (k + t - 1) + stream][way] for way in range(2) for t in range(1, col_size)
        ]
        gate = [products[max(q - 2, min(q - 1, 1))]] if q > 0 else []
        flat = lax.optimization_barrier((*flat, *gate))
        own = pick(
            meta, panels, k, stream, [flat[: col_size - 1], flat[col_size - 1 : 2 * (col_size - 1)]]
        )
        picked.append((own, swap(own, 1, row_size)))

    def arrive(n):
        nonlocal done
        while done < 2 * supernodes:
            need = min(done + 1, 2 * supernodes - 1) if done > 1 else done
            if 2 * (need // 2 + col_size - 2) + need % 2 > n:
                break
            while len(picked) <= need:
                pick_now(len(picked))
            k, stream = done // 2, done % 2
            own, oth = picked[done]
            if need > done:
                own = after(own, *[pair[0] for pair in picked[done + 1 : need + 1]])
            link = None if k == 0 else link_full[k - 1]
            ties = products[-1:] or [link_full]
            if k == supernodes - 1 and k > 1:
                ties = ties + ([sums[0]] if stream == 0 else summed[0][:2])
            if ties:
                own = after(own, *ties)
            if stream == 0:
                products.append(panel_first(meta, inverse_block, own, oth))
            else:
                part, right, left = panel_second(
                    meta, inverse_block, own, oth, products[-1], link,
                    parts[-1] if k > 0 else None, col_size,
                )
                parts.append(part)
                products.append(part)
                hops.append([(shift(right, 1, col_size), shift(left, -1, col_size))])
            for k in range(supernodes):
                if done == min(2 * k + 2, 2 * supernodes - 1):
                    scatter(k)
            if done == 3 and supernodes > 2:
                finish(0, products[-1:])
            done += 1

    for step in range(steps):
        for stream in range(STREAMS):
            arrived = events[-STREAMS] if step > 0 else []
            if step < supernodes:
                values = feed(meta, panels, step, stream, arrived)
            else:
                values = arrived
            tie = events[-STREAMS - 1] if len(events) > STREAMS else []
            if len(events) == 2 * col_size - 1:
                tie = tie + products[:1]
            elif len(events) == 2 * col_size + 1:
                tie = tie + products[1:2]
            values = lax.optimization_barrier((*values, *tie))[: len(orders)]
            events.append(send_on(values, orders, step, supernodes))
            if len(events) == 2:
                flat = after(links, *events[0]).reshape(-1, width)
                half = flat.shape[0] // 2
                my_links = lax.dynamic_slice_in_dim(flat, lane * half, half, 0)
                got = around([my_links] + [shift(my_links, s, col_size) for s in range(1, col_size)], col_number)
                link_full = both_halves(got, lane, row_size, 1)
                link_full = link_full.reshape(col_size, supernodes - 1, -1, width)
                link_full = link_full.transpose(1, 0, 2, 3).reshape(supernodes - 1, width, width)
            arrive(len(events) - 1)
    for k in range(supernodes):
        last = k + 1 == supernodes
        if last:
            finish(k)
        elif k > 0:
            finish(k, hops[-1][min(1, len(hops[-1]) - 1)], ((), hops[-1][-1]))
        link = None if k == 0 else link_full[k - 1]
        total = summed[k][-1]
        mine = lax.dynamic_slice_in_dim(diag_inverse[k], lane * (share // 2), share // 2, 1).T
        turned = mine - total[:, :width]
        if k > 0:
            link_wide = link.astype(f32)
            link_share = lax.dynamic_slice_in_dim(link_wide, col_number * share, share, 1)
            cross = -(stacked + turned_product(full_turned, link_share))
            cross_parts.append(cross)
            cross_half = lax.dynamic_slice_in_dim(cross, lane * (share // 2), share // 2, 1)
            turned = turned - turned_product(cross_half, link_wide)
        if last:
            diag_parts.append(both_halves(turned, lane, row_size, 0).T)
        else:
            arrived = []
            for s in range(col_size):
                at = (col_number + s) % col_size * share
                block = lax.dynamic_slice_in_dim(total[:, width:], at, share, 1)
                message = jnp.concatenate([turned, block], axis=1)
                arrived.append(shift(message, s, col_size) if s else message)
            if k + 2 < supernodes:
                arrived = after(tuple(arrived), *hops[-1][min(1, len(hops[-1]) - 1)])
            ordered = around(list(arrived), col_number)
            ordered = both_halves(ordered, lane, row_size, 1)
            full_turned = ordered[:, :, :width].reshape(width, width)
            stacked = ordered[:, :, width:].reshape(width, share)
            diag_parts.append(
                lax.dynamic_slice_in_dim(full_turned, col_number * share, share, 0).T
            )
    return carried, jnp.stack(cross_parts), jnp.stack(diag_parts)


def solution(mesh):
    in_specs = (
        P("row", "col"),
        P(),
        P(None, "row", None),
        P(None, "col", None),
        P(None, None, "col"),
    )
    out_specs = (P(None, "row", "col"), P(None, None, "col"), P(None, None, "col"))
    return jax.shard_map(local, mesh=mesh, in_specs=in_specs, out_specs=out_specs, check_vma=False)
```

```python
import functools

import jax
import jax.numpy as jnp
from jax import lax
from jax.experimental import pallas as pl
from jax.experimental.pallas import tpu as pltpu
from jax.sharding import PartitionSpec as P

TILE = 256
PAD = 16
LANES = 2
STREAMS = 2
FEED_COST = 10_000_000_000
VMEM = 24 << 20
HEAD = 4

precise = lax.Precision.HIGHEST
f32 = jnp.float32
bf16 = jnp.bfloat16
i16 = jnp.int16
BOTH = ("row", "col")


def product(left, right):
    return jnp.dot(left, right, precision=precise, preferred_element_type=f32)


def turned_product(left, right):
    return lax.dot_general(
        left, right, (((0,), (0,)), ((), ())), precision=precise, preferred_element_type=f32
    )


def split_dot(value, right):
    high = value.astype(bf16)
    low = (value - high.astype(f32)).astype(bf16)
    return jnp.dot(high, right, preferred_element_type=f32) + jnp.dot(
        low, right, preferred_element_type=f32
    )


def shift(value, by, size):
    return lax.ppermute(value, "col", [(z, (z + by) % size) for z in range(size)])


def swap(value, bit, size):
    return lax.ppermute(value, "row", [(r, r ^ bit) for r in range(size)])


def quantize(value):
    top = jnp.max(jnp.abs(value), axis=0, keepdims=True)
    power = jnp.clip(jnp.ceil(jnp.log2(jnp.maximum(top, 1e-30))), -100.0, 100.0)
    scaled = jnp.clip(jnp.round(value * jnp.exp2(15.0 - power)), -32767.0, 32767.0)
    return scaled.astype(jnp.int32).astype(i16), power.astype(jnp.int32)


def restore(ref, at, tile):
    count = ref.shape[0] - PAD
    powers = ref[count:, :].astype(jnp.int32).astype(f32)
    scale = jnp.exp2(powers[tile : tile + 1, :] - 15.0)
    return ref[at : at + TILE, :].astype(jnp.int32).astype(f32) * scale


def first_kernel(meta, s_own, s_oth, own, oth, total):
    @pl.when(meta[HEAD + pl.program_id(0)] > 0)
    def _():
        total[...] = split_dot(s_own[...], own[...]) + split_dot(s_oth[...], oth[...])


def second_kernel(cols, chained, meta, s_own, s_oth, own, oth, before, *rest):
    rest = list(rest)
    if chained:
        link, prev = rest[:2]
        rest = rest[2:]
    part, out_a, out_b, powers = rest
    step = pl.program_id(0)
    tiles = pl.num_programs(0)
    share = part.shape[2]
    half = out_a.shape[0] - PAD
    far = lax.rem(meta[1] + cols // 2, cols)

    @pl.when(step == 0)
    def _():
        powers[...] = jnp.zeros_like(powers)

    def put(quant):
        at = step * TILE

        @pl.when(at < half)
        def _():
            out_a[pl.ds(pl.multiple_of(at, TILE), TILE), :] = quant

        @pl.when(at >= half)
        def _():
            out_b[pl.ds(pl.multiple_of(at - half, TILE), TILE), :] = quant

    listed = meta[HEAD + step] > 0

    @pl.when(listed)
    def _():
        total = before[...] + split_dot(s_own[...], own[...]) + split_dot(s_oth[...], oth[...])
        if chained:
            earlier = jnp.concatenate([prev[j] for j in range(cols)], axis=1)
            total = total + split_dot(earlier, link[...])
        for j in range(cols):
            part[j] = -total[:, j * share : (j + 1) * share]
        quant, power = quantize(part[far])
        put(quant)
        spot = lax.broadcasted_iota(jnp.int32, powers.shape, 0) == step
        powers[...] = jnp.where(spot, jnp.broadcast_to(power, powers.shape), powers[...])

    @pl.when(jnp.logical_not(listed))
    def _():
        part[...] = jnp.zeros_like(part)
        put(jnp.zeros((TILE, share), i16))

    @pl.when(step == tiles - 1)
    def _():
        out_a[half:, :] = powers[...].astype(i16)
        out_b[out_b.shape[0] - PAD :, :] = powers[...].astype(i16)


def panel_specs(rows, depth, width, stream):
    block = rows // STREAMS
    by_lane = lambda i, m: (i, m[0] * STREAMS + stream)
    by_other = lambda i, m: (i, (1 - m[0]) * STREAMS + stream)
    whole = lambda i, m: (0, 0)
    return [
        pl.BlockSpec((TILE, block), by_lane),
        pl.BlockSpec((TILE, block), by_other),
        pl.BlockSpec((block, width), whole),
        pl.BlockSpec((block, width), whole),
    ]


def panel_first(meta, matrix, own, oth):
    rows, depth = matrix.shape
    width = own.shape[1]
    return pl.pallas_call(
        first_kernel,
        grid_spec=pltpu.PrefetchScalarGridSpec(
            num_scalar_prefetch=1,
            grid=(rows // TILE,),
            in_specs=panel_specs(rows, depth, width, 0),
            out_specs=pl.BlockSpec((TILE, width), lambda i, m: (i, 0)),
        ),
        out_shape=jax.ShapeDtypeStruct((rows, width), f32),
        compiler_params=pltpu.CompilerParams(vmem_limit_bytes=VMEM),
        cost_estimate=pl.CostEstimate(
            flops=2 * rows * depth * width, bytes_accessed=2 * rows * depth, transcendentals=0
        ),
    )(meta, matrix, matrix, own, oth)


def panel_second(meta, matrix, own, oth, before, link, prev, cols):
    rows, depth = matrix.shape
    width = own.shape[1]
    share = width // cols
    half = rows // 2
    whole = lambda i, m: (0, 0)
    tile_of = pl.BlockSpec((cols, TILE, share), lambda i, m: (0, i, 0))
    in_specs = panel_specs(rows, depth, width, 1) + [pl.BlockSpec((TILE, width), lambda i, m: (i, 0))]
    operands = [matrix, matrix, own, oth, before]
    if link is not None:
        in_specs += [pl.BlockSpec((width, width), whole), tile_of]
        operands += [link, prev]
    message = jax.ShapeDtypeStruct((half + PAD, share), i16)
    return pl.pallas_call(
        functools.partial(second_kernel, cols, link is not None),
        grid_spec=pltpu.PrefetchScalarGridSpec(
            num_scalar_prefetch=1,
            grid=(rows // TILE,),
            in_specs=in_specs,
            out_specs=[tile_of] + [pl.BlockSpec((half + PAD, share), whole)] * 2,
            scratch_shapes=[pltpu.VMEM((PAD, share), jnp.int32)],
        ),
        out_shape=[jax.ShapeDtypeStruct((cols, rows, share), f32), message, message],
        compiler_params=pltpu.CompilerParams(vmem_limit_bytes=VMEM),
        cost_estimate=pl.CostEstimate(
            flops=2 * rows * depth * width, bytes_accessed=2 * rows * depth, transcendentals=0
        ),
    )(meta, *operands)


def pass_kernel(meta, right, left, got_right, got_left, out_right, out_left):
    rows = right.shape[1]
    spot = lax.broadcasted_iota(jnp.int32, (PAD, right.shape[2]), 0)
    for mine, got, out, low in ((right, got_right, out_right, True), (left, got_left, out_left, False)):
        count = got.shape[0] - PAD
        begin = 0 if low else rows - count
        powers = jnp.zeros(spot.shape, jnp.int32)
        for tile in range(rows // TILE):
            at = tile * TILE
            total = mine[0, at : at + TILE, :]
            if begin <= at < begin + count:
                total = total + restore(got, at - begin, tile)
            quant, power = quantize(total)
            out[at : at + TILE, :] = quant
            powers = jnp.where(spot == tile, jnp.broadcast_to(power, spot.shape), powers)
        out[rows:, :] = powers.astype(i16)


def pass_on(meta, part, got_right, got_left, hop):
    cols, rows, share = part.shape
    everything = lambda i, m: (0, 0)
    message = jax.ShapeDtypeStruct((rows + PAD, share), i16)
    return pl.pallas_call(
        pass_kernel,
        grid_spec=pltpu.PrefetchScalarGridSpec(
            num_scalar_prefetch=1,
            grid=(1,),
            in_specs=[
                pl.BlockSpec((1, rows, share), lambda i, m: (lax.rem(m[1] + hop, cols), 0, 0)),
                pl.BlockSpec((1, rows, share), lambda i, m: (lax.rem(m[1] + cols - hop, cols), 0, 0)),
                pl.BlockSpec(got_right.shape, everything),
                pl.BlockSpec(got_left.shape, everything),
            ],
            out_specs=[pl.BlockSpec((rows + PAD, share), everything)] * 2,
        ),
        out_shape=[message, message],
        compiler_params=pltpu.CompilerParams(vmem_limit_bytes=VMEM),
    )(meta, part, part, got_right, got_left)


def sum_kernel(tiles, count, meta, mine, got_right, got_left, *rest):
    factors = rest[:count]
    x_ref, sums = rest[-2:]
    step = pl.program_id(0)

    @pl.when(step == 0)
    def _():
        sums[...] = jnp.zeros_like(sums)

    for tile in range(tiles):

        @pl.when(step == tile)
        def _(tile=tile):
            total = mine[0]
            for got, low in ((got_right, True), (got_left, False)):
                rows = got.shape[0] - PAD
                begin = 0 if low else tiles * TILE - rows
                if begin <= tile * TILE < begin + rows:
                    total = total + restore(got, tile * TILE - begin, tile)
            x_ref[0] = total

    turned = x_ref[0].T
    width = factors[0].shape[2]
    for n, factor in enumerate(factors):
        sums[:, n * width : (n + 1) * width] += split_dot(turned, factor[0])


def sum_parts(meta, part, got_right, got_left, panels, k, carried):
    cols, rows, share = part.shape
    supernodes, _, width = panels.shape
    tiles = rows // TILE
    count = 1 if k + 1 == supernodes else 2
    everything = lambda i, m: (0, 0)
    in_specs = [
        pl.BlockSpec((1, TILE, share), lambda i, m: (m[1], i, 0)),
        pl.BlockSpec(got_right.shape, everything),
        pl.BlockSpec(got_left.shape, everything),
    ] + [pl.BlockSpec((1, TILE, width), lambda i, m, n=n: (k + n, i, 0)) for n in range(count)]
    operands = [part, got_right, got_left] + [panels] * count
    aliases = {}
    if carried is not None:
        in_specs.append(pl.BlockSpec(memory_space=pl.ANY))
        operands.append(carried)
        aliases = {len(operands): 0}
    return pl.pallas_call(
        functools.partial(sum_kernel, tiles, count),
        grid_spec=pltpu.PrefetchScalarGridSpec(
            num_scalar_prefetch=1,
            grid=(tiles,),
            in_specs=in_specs,
            out_specs=[
                pl.BlockSpec((1, TILE, share), lambda i, m: (k, i, 0)),
                pl.BlockSpec((share, count * width), everything),
            ],
        ),
        out_shape=[
            jax.ShapeDtypeStruct((supernodes, rows, share), f32),
            jax.ShapeDtypeStruct((share, count * width), f32),
        ],
        input_output_aliases=aliases,
        compiler_params=pltpu.CompilerParams(vmem_limit_bytes=VMEM),
    )(meta, *operands)


def around(pieces, col_number):
    size = len(pieces)
    ring = jnp.stack(pieces[::-1] + pieces[:0:-1])
    return lax.dynamic_slice_in_dim(ring, size - 1 - col_number, size, 0)


def row_sum_half(value, lane, row_size, gates=()):
    half = value.shape[0] // 2
    keep = lax.dynamic_slice_in_dim(value, lane * half, half, 0)
    give = lax.dynamic_slice_in_dim(value, (1 - lane) * half, half, 0)
    stages = [keep + swap(give, 1, row_size)]
    bit = 2
    while bit < row_size:
        value = stages[-1]
        if len(stages) <= len(gates):
            value = after(value, *gates[len(stages) - 1])
        stages.append(value + swap(value, bit, row_size))
        bit *= 2
    return stages


def both_halves(half, lane, row_size, axis):
    other = swap(half, 1, row_size)
    pick = lane == 0
    return jnp.concatenate(
        [jnp.where(pick, half, other), jnp.where(pick, other, half)], axis=axis
    )


def after(value, *others):
    return lax.optimization_barrier((value, *others))[0]


def own_blocks(meta, row, rows):
    block = min(rows, TILE)
    return [(at, block, meta[HEAD + (row + at) // TILE]) for at in range(0, rows, block)]


def feed_kernel(spots, meta, *refs):
    ways = len(spots)
    own, outs = refs[:ways], refs[-ways:]
    arrived = refs[ways:-ways]
    for way, row in enumerate(spots):
        out = outs[way]

        def fill(way=way, row=row, out=out):
            for at, block, flag in own_blocks(meta, row, out.shape[0]):
                value = own[way][0, at : at + block, :]
                out[at : at + block, :] = jnp.where(flag > 0, value, jnp.zeros_like(value))

        if not arrived:
            fill()
        else:
            first = meta[2 + way] == 0
            pl.when(first)(fill)

            @pl.when(jnp.logical_not(first))
            def _(way=way, out=out):
                out[...] = arrived[way][...]


def feed(meta, panels, k, stream, arrived):
    _, rows, width = panels.shape
    ways = 2
    piece = rows // (ways * STREAMS)
    block = pl.BlockSpec((piece, width), lambda i, m: (0, 0))
    return pl.pallas_call(
        functools.partial(feed_kernel, [(stream * ways + way) * piece for way in range(ways)]),
        grid_spec=pltpu.PrefetchScalarGridSpec(
            num_scalar_prefetch=1,
            grid=(1,),
            in_specs=[
                pl.BlockSpec((1, piece, width), lambda i, m, w=w: (k, stream * ways + w, 0))
                for w in range(ways)
            ]
            + [block] * len(arrived),
            out_specs=[block] * ways,
        ),
        out_shape=[jax.ShapeDtypeStruct((piece, width), bf16)] * ways,
        compiler_params=pltpu.CompilerParams(vmem_limit_bytes=VMEM),
        cost_estimate=pl.CostEstimate(flops=FEED_COST, bytes_accessed=0, transcendentals=0),
    )(meta, *[panels] * ways, *arrived)


def pick_kernel(k, spots, meta, panels, *refs):
    ways = len(spots)
    out, sems = refs[-2:]
    turns = len(refs[:-2]) // ways
    piece = out.shape[0] // ways

    def each(act):
        for way, row in enumerate(spots):
            base = way * piece
            turn = meta[2 + way]
            for t in range(turns):

                @pl.when(turn == t + 1)
                def _(way=way, t=t, base=base):
                    target = out.at[pl.ds(base, piece)]
                    act(pltpu.make_async_copy(refs[way * turns + t], target, sems.at[way, 0]))

            for n, (at, block, flag) in enumerate(own_blocks(meta, row, piece)):
                target = out.at[pl.ds(base + at, block)]

                @pl.when((turn == 0) & (flag > 0))
                def _(way=way, n=n, row=row, at=at, block=block, target=target):
                    source = panels.at[k, pl.ds(row + at, block)]
                    act(pltpu.make_async_copy(source, target, sems.at[way, n]))


    each(lambda copy: copy.start())
    for way, row in enumerate(spots):
        for at, block, flag in own_blocks(meta, row, piece):

            @pl.when((meta[2 + way] == 0) & (flag == 0))
            def _(at=way * piece + at, block=block):
                out[at : at + block, :] = jnp.zeros((block, out.shape[1]), out.dtype)

    each(lambda copy: copy.wait())


def pick(meta, panels, k, stream, received):
    _, rows, width = panels.shape
    ways = len(received)
    piece = rows // (ways * STREAMS)
    block = min(piece, TILE)
    operands = [panels] + [value for way in received for value in way]
    return pl.pallas_call(
        functools.partial(pick_kernel, k, [(stream * ways + way) * piece for way in range(ways)]),
        grid_spec=pltpu.PrefetchScalarGridSpec(
            num_scalar_prefetch=1,
            grid=(1,),
            in_specs=[pl.BlockSpec(memory_space=pltpu.HBM)] * len(operands),
            out_specs=pl.BlockSpec((ways * piece, width), lambda i, m: (0, 0)),
            scratch_shapes=[pltpu.SemaphoreType.DMA((ways, piece // block))],
        ),
        out_shape=jax.ShapeDtypeStruct((ways * piece, width), bf16),
        compiler_params=pltpu.CompilerParams(vmem_limit_bytes=VMEM),
    )(meta, *operands)


def send_on(values, orders, step, supernodes):
    size = len(orders[0])
    got = []
    for value, order in zip(values, orders):
        pairs = []
        for t in range(size - 1):
            if 0 <= step - t < supernodes:
                for c in range(size):
                    for i in range(LANES):
                        source = ((c ^ order[t]) * LANES + i) * size + c
                        target = ((c ^ order[t + 1]) * LANES + i) * size + c
                        pairs.append((source, target))
        got.append(lax.ppermute(value, BOTH, pairs))
    return got


def local(inverse_block, tile_list, panels, links, diag_inverse):
    rows_here = inverse_block.shape[0]
    share = diag_inverse.shape[2]
    row_size, col_size = lax.axis_size("row"), lax.axis_size("col")
    row_number, col_number = lax.axis_index("row"), lax.axis_index("col")
    place, lane = row_number // LANES, row_number % LANES
    supernodes, _, width = panels.shape
    tiles_here = rows_here // TILE
    tiles = row_number * tiles_here + jnp.arange(tiles_here, dtype=jnp.int32)
    flags = jnp.any(tile_list[None, :] == tiles[:, None], axis=1)

    order = [t ^ (t >> 1) for t in range(col_size)]
    back = [order[-t] for t in range(col_size)]
    orders = (order, back)
    relative = place ^ col_number
    turn = sum(jnp.where(relative == order[t], t, 0) for t in range(col_size))
    meta = jnp.concatenate(
        [
            jnp.stack([lane, col_number, turn, (col_size - turn) % col_size]).astype(jnp.int32),
            flags.astype(jnp.int32),
        ]
    )

    cross_parts, diag_parts = [], []
    carried = cross = stacked = full_turned = None
    link_full = None
    events = []
    steps = supernodes + col_size - 2
    parts, products, hops, sums, summed = [], [], [], [], []
    done = 0

    picked = []

    def finish(k, ties=(), gates=()):
        nonlocal carried
        right, left = hops[k][-1]
        if ties:
            right = after(right, *ties)
        carried, total = sum_parts(meta, parts[k], right, left, panels, k, carried)
        sums.append(total)
        summed.append(row_sum_half(total, lane, row_size, gates))

    def scatter(k):
        right, left = hops[k][-1]
        for hop in range(col_size // 2 - 1, 0, -1):
            right = after(right, products[-1])
            right, left = pass_on(meta, parts[k], right, left, hop)
            hops[k].append((right, left))
            right, left = shift(right, 1, col_size), shift(left, -1, col_size)
            hops[k].append((right, left))

    def pick_now(q):
        k, stream = q // 2, q % 2
        flat = [
            events[2 * (k + t - 1) + stream][way] for way in range(2) for t in range(1, col_size)
        ]
        gate = [products[max(q - 2, min(q - 1, 1))]] if q > 0 else []
        flat = lax.optimization_barrier((*flat, *gate))
        own = pick(
            meta, panels, k, stream, [flat[: col_size - 1], flat[col_size - 1 : 2 * (col_size - 1)]]
        )
        picked.append((own, swap(own, 1, row_size)))

    def arrive(n):
        nonlocal done
        while done < 2 * supernodes:
            need = min(done + 1, 2 * supernodes - 1) if done > 1 else done
            if 2 * (need // 2 + col_size - 2) + need % 2 > n:
                break
            while len(picked) <= need:
                pick_now(len(picked))
            k, stream = done // 2, done % 2
            own, oth = picked[done]
            if need > done:
                own = after(own, *[pair[0] for pair in picked[done + 1 : need + 1]])
            link = None if k == 0 else link_full[k - 1]
            ties = products[-1:] or [link_full]
            if k == supernodes - 1 and k > 1:
                ties = ties + ([sums[0]] if stream == 0 else summed[0][:2])
            if ties:
                own = after(own, *ties)
            if stream == 0:
                products.append(panel_first(meta, inverse_block, own, oth))
            else:
                part, right, left = panel_second(
                    meta, inverse_block, own, oth, products[-1], link,
                    parts[-1] if k > 0 else None, col_size,
                )
                parts.append(part)
                products.append(part)
                hops.append([(shift(right, 1, col_size), shift(left, -1, col_size))])
            for k in range(supernodes):
                if done == min(2 * k + 2, 2 * supernodes - 1):
                    scatter(k)
            if done == 3 and supernodes > 2:
                finish(0, products[-1:])
            done += 1

    for step in range(steps):
        for stream in range(STREAMS):
            arrived = events[-STREAMS] if step > 0 else []
            if step < supernodes:
                values = feed(meta, panels, step, stream, arrived)
            else:
                values = arrived
            tie = events[-STREAMS - 1] if len(events) > STREAMS else []
            if len(events) == 2 * col_size - 1:
                tie = tie + products[:1]
            elif len(events) == 2 * col_size + 1:
                tie = tie + products[1:2]
            values = lax.optimization_barrier((*values, *tie))[: len(orders)]
            events.append(send_on(values, orders, step, supernodes))
            if len(events) == 2:
                flat = after(links, *events[0]).reshape(-1, width)
                half = flat.shape[0] // 2
                my_links = lax.dynamic_slice_in_dim(flat, lane * half, half, 0)
                got = around([my_links] + [shift(my_links, s, col_size) for s in range(1, col_size)], col_number)
                link_full = both_halves(got, lane, row_size, 1)
                link_full = link_full.reshape(col_size, supernodes - 1, -1, width)
                link_full = link_full.transpose(1, 0, 2, 3).reshape(supernodes - 1, width, width)
            arrive(len(events) - 1)
    for k in range(supernodes):
        last = k + 1 == supernodes
        if k == 0:
            for later in range(1, supernodes):
                if later + 1 < supernodes:
                    stages = hops[-1]
                    finish(later, stages[min(1, len(stages) - 1)], ((), stages[-1]))
                else:
                    finish(later)
        link = None if k == 0 else link_full[k - 1]
        total = summed[k][-1]
        mine = lax.dynamic_slice_in_dim(diag_inverse[k], lane * (share // 2), share // 2, 1).T
        turned = mine - total[:, :width]
        if k > 0:
            link_wide = link.astype(f32)
            link_share = lax.dynamic_slice_in_dim(link_wide, col_number * share, share, 1)
            cross = -(stacked + turned_product(full_turned, link_share))
            cross_parts.append(cross)
            cross_half = lax.dynamic_slice_in_dim(cross, lane * (share // 2), share // 2, 1)
            turned = turned - turned_product(cross_half, link_wide)
        if last:
            diag_parts.append(both_halves(turned, lane, row_size, 0).T)
        else:
            arrived = []
            for s in range(col_size):
                at = (col_number + s) % col_size * share
                block = lax.dynamic_slice_in_dim(total[:, width:], at, share, 1)
                message = jnp.concatenate([turned, block], axis=1)
                arrived.append(shift(message, s, col_size) if s else message)
            if k + 2 < supernodes:
                arrived = after(tuple(arrived), sums[-1])
            ordered = around(list(arrived), col_number)
            ordered = both_halves(ordered, lane, row_size, 1)
            full_turned = ordered[:, :, :width].reshape(width, width)
            stacked = ordered[:, :, width:].reshape(width, share)
            diag_parts.append(
                lax.dynamic_slice_in_dim(full_turned, col_number * share, share, 0).T
            )
    return carried, jnp.stack(cross_parts), jnp.stack(diag_parts)


def solution(mesh):
    in_specs = (
        P("row", "col"),
        P(),
        P(None, "row", None),
        P(None, "col", None),
        P(None, None, "col"),
    )
    out_specs = (P(None, "row", "col"), P(None, None, "col"), P(None, None, "col"))
    return jax.shard_map(local, mesh=mesh, in_specs=in_specs, out_specs=out_specs, check_vma=False)
```

```python
import functools

import jax
import jax.numpy as jnp
from jax import lax
from jax.experimental import pallas as pl
from jax.experimental.pallas import tpu as pltpu
from jax.sharding import PartitionSpec as P

TILE = 256
PAD = 16
LANES = 2
STREAMS = 2
FEED_COST = 10_000_000_000
VMEM = 24 << 20
HEAD = 4

precise = lax.Precision.HIGHEST
f32 = jnp.float32
bf16 = jnp.bfloat16
i16 = jnp.int16
BOTH = ("row", "col")


def product(left, right):
    return jnp.dot(left, right, precision=precise, preferred_element_type=f32)


def turned_product(left, right):
    return lax.dot_general(
        left, right, (((0,), (0,)), ((), ())), precision=precise, preferred_element_type=f32
    )


def split_dot(value, right):
    high = value.astype(bf16)
    low = (value - high.astype(f32)).astype(bf16)
    return jnp.dot(high, right, preferred_element_type=f32) + jnp.dot(
        low, right, preferred_element_type=f32
    )


def shift(value, by, size):
    return lax.ppermute(value, "col", [(z, (z + by) % size) for z in range(size)])


def swap(value, bit, size):
    return lax.ppermute(value, "row", [(r, r ^ bit) for r in range(size)])


def quantize(value):
    top = jnp.max(jnp.abs(value), axis=0, keepdims=True)
    power = jnp.clip(jnp.ceil(jnp.log2(jnp.maximum(top, 1e-30))), -100.0, 100.0)
    scaled = jnp.clip(jnp.round(value * jnp.exp2(15.0 - power)), -32767.0, 32767.0)
    return scaled.astype(jnp.int32).astype(i16), power.astype(jnp.int32)


def restore(ref, at, tile):
    count = ref.shape[0] - PAD
    powers = ref[count:, :].astype(jnp.int32).astype(f32)
    scale = jnp.exp2(powers[tile : tile + 1, :] - 15.0)
    return ref[at : at + TILE, :].astype(jnp.int32).astype(f32) * scale


def first_kernel(meta, s_own, s_oth, own, oth, total):
    @pl.when(meta[HEAD + pl.program_id(0)] > 0)
    def _():
        total[...] = split_dot(s_own[...], own[...]) + split_dot(s_oth[...], oth[...])


def second_kernel(cols, chained, meta, s_own, s_oth, own, oth, before, *rest):
    rest = list(rest)
    if chained:
        link, prev = rest[:2]
        rest = rest[2:]
    part, out_a, out_b, powers = rest
    step = pl.program_id(0)
    tiles = pl.num_programs(0)
    share = part.shape[2]
    half = out_a.shape[0] - PAD
    far = lax.rem(meta[1] + cols // 2, cols)

    @pl.when(step == 0)
    def _():
        powers[...] = jnp.zeros_like(powers)

    def put(quant):
        at = step * TILE

        @pl.when(at < half)
        def _():
            out_a[pl.ds(pl.multiple_of(at, TILE), TILE), :] = quant

        @pl.when(at >= half)
        def _():
            out_b[pl.ds(pl.multiple_of(at - half, TILE), TILE), :] = quant

    listed = meta[HEAD + step] > 0

    @pl.when(listed)
    def _():
        total = before[...] + split_dot(s_own[...], own[...]) + split_dot(s_oth[...], oth[...])
        if chained:
            earlier = jnp.concatenate([prev[j] for j in range(cols)], axis=1)
            total = total + split_dot(earlier, link[...])
        for j in range(cols):
            part[j] = -total[:, j * share : (j + 1) * share]
        quant, power = quantize(part[far])
        put(quant)
        spot = lax.broadcasted_iota(jnp.int32, powers.shape, 0) == step
        powers[...] = jnp.where(spot, jnp.broadcast_to(power, powers.shape), powers[...])

    @pl.when(jnp.logical_not(listed))
    def _():
        part[...] = jnp.zeros_like(part)
        put(jnp.zeros((TILE, share), i16))

    @pl.when(step == tiles - 1)
    def _():
        out_a[half:, :] = powers[...].astype(i16)
        out_b[out_b.shape[0] - PAD :, :] = powers[...].astype(i16)


def panel_specs(rows, depth, width, stream):
    block = rows // STREAMS
    by_lane = lambda i, m: (i, m[0] * STREAMS + stream)
    by_other = lambda i, m: (i, (1 - m[0]) * STREAMS + stream)
    whole = lambda i, m: (0, 0)
    return [
        pl.BlockSpec((TILE, block), by_lane),
        pl.BlockSpec((TILE, block), by_other),
        pl.BlockSpec((block, width), whole),
        pl.BlockSpec((block, width), whole),
    ]


def panel_first(meta, matrix, own, oth):
    rows, depth = matrix.shape
    width = own.shape[1]
    return pl.pallas_call(
        first_kernel,
        grid_spec=pltpu.PrefetchScalarGridSpec(
            num_scalar_prefetch=1,
            grid=(rows // TILE,),
            in_specs=panel_specs(rows, depth, width, 0),
            out_specs=pl.BlockSpec((TILE, width), lambda i, m: (i, 0)),
        ),
        out_shape=jax.ShapeDtypeStruct((rows, width), f32),
        compiler_params=pltpu.CompilerParams(vmem_limit_bytes=VMEM),
        cost_estimate=pl.CostEstimate(
            flops=2 * rows * depth * width, bytes_accessed=2 * rows * depth, transcendentals=0
        ),
    )(meta, matrix, matrix, own, oth)


def panel_second(meta, matrix, own, oth, before, link, prev, cols):
    rows, depth = matrix.shape
    width = own.shape[1]
    share = width // cols
    half = rows // 2
    whole = lambda i, m: (0, 0)
    tile_of = pl.BlockSpec((cols, TILE, share), lambda i, m: (0, i, 0))
    in_specs = panel_specs(rows, depth, width, 1) + [pl.BlockSpec((TILE, width), lambda i, m: (i, 0))]
    operands = [matrix, matrix, own, oth, before]
    if link is not None:
        in_specs += [pl.BlockSpec((width, width), whole), tile_of]
        operands += [link, prev]
    message = jax.ShapeDtypeStruct((half + PAD, share), i16)
    return pl.pallas_call(
        functools.partial(second_kernel, cols, link is not None),
        grid_spec=pltpu.PrefetchScalarGridSpec(
            num_scalar_prefetch=1,
            grid=(rows // TILE,),
            in_specs=in_specs,
            out_specs=[tile_of] + [pl.BlockSpec((half + PAD, share), whole)] * 2,
            scratch_shapes=[pltpu.VMEM((PAD, share), jnp.int32)],
        ),
        out_shape=[jax.ShapeDtypeStruct((cols, rows, share), f32), message, message],
        compiler_params=pltpu.CompilerParams(vmem_limit_bytes=VMEM),
        cost_estimate=pl.CostEstimate(
            flops=2 * rows * depth * width, bytes_accessed=2 * rows * depth, transcendentals=0
        ),
    )(meta, *operands)


def pass_kernel(meta, right, left, got_right, got_left, out_right, out_left):
    rows = right.shape[1]
    spot = lax.broadcasted_iota(jnp.int32, (PAD, right.shape[2]), 0)
    for mine, got, out, low in ((right, got_right, out_right, True), (left, got_left, out_left, False)):
        count = got.shape[0] - PAD
        begin = 0 if low else rows - count
        powers = jnp.zeros(spot.shape, jnp.int32)
        for tile in range(rows // TILE):
            at = tile * TILE
            total = mine[0, at : at + TILE, :]
            if begin <= at < begin + count:
                total = total + restore(got, at - begin, tile)
            quant, power = quantize(total)
            out[at : at + TILE, :] = quant
            powers = jnp.where(spot == tile, jnp.broadcast_to(power, spot.shape), powers)
        out[rows:, :] = powers.astype(i16)


def pass_on(meta, part, got_right, got_left, hop):
    cols, rows, share = part.shape
    everything = lambda i, m: (0, 0)
    message = jax.ShapeDtypeStruct((rows + PAD, share), i16)
    return pl.pallas_call(
        pass_kernel,
        grid_spec=pltpu.PrefetchScalarGridSpec(
            num_scalar_prefetch=1,
            grid=(1,),
            in_specs=[
                pl.BlockSpec((1, rows, share), lambda i, m: (lax.rem(m[1] + hop, cols), 0, 0)),
                pl.BlockSpec((1, rows, share), lambda i, m: (lax.rem(m[1] + cols - hop, cols), 0, 0)),
                pl.BlockSpec(got_right.shape, everything),
                pl.BlockSpec(got_left.shape, everything),
            ],
            out_specs=[pl.BlockSpec((rows + PAD, share), everything)] * 2,
        ),
        out_shape=[message, message],
        compiler_params=pltpu.CompilerParams(vmem_limit_bytes=VMEM),
    )(meta, part, part, got_right, got_left)


def sum_kernel(tiles, count, meta, mine, got_right, got_left, *rest):
    factors = rest[:count]
    x_ref, sums = rest[-2:]
    step = pl.program_id(0)

    @pl.when(step == 0)
    def _():
        sums[...] = jnp.zeros_like(sums)

    for tile in range(tiles):

        @pl.when(step == tile)
        def _(tile=tile):
            total = mine[0]
            for got, low in ((got_right, True), (got_left, False)):
                rows = got.shape[0] - PAD
                begin = 0 if low else tiles * TILE - rows
                if begin <= tile * TILE < begin + rows:
                    total = total + restore(got, tile * TILE - begin, tile)
            x_ref[0] = total

    turned = x_ref[0].T
    width = factors[0].shape[2]
    for n, factor in enumerate(factors):
        sums[:, n * width : (n + 1) * width] += split_dot(turned, factor[0])


def sum_parts(meta, part, got_right, got_left, panels, k, carried):
    cols, rows, share = part.shape
    supernodes, _, width = panels.shape
    tiles = rows // TILE
    count = 1 if k + 1 == supernodes else 2
    everything = lambda i, m: (0, 0)
    in_specs = [
        pl.BlockSpec((1, TILE, share), lambda i, m: (m[1], i, 0)),
        pl.BlockSpec(got_right.shape, everything),
        pl.BlockSpec(got_left.shape, everything),
    ] + [pl.BlockSpec((1, TILE, width), lambda i, m, n=n: (k + n, i, 0)) for n in range(count)]
    operands = [part, got_right, got_left] + [panels] * count
    aliases = {}
    if carried is not None:
        in_specs.append(pl.BlockSpec(memory_space=pl.ANY))
        operands.append(carried)
        aliases = {len(operands): 0}
    return pl.pallas_call(
        functools.partial(sum_kernel, tiles, count),
        grid_spec=pltpu.PrefetchScalarGridSpec(
            num_scalar_prefetch=1,
            grid=(tiles,),
            in_specs=in_specs,
            out_specs=[
                pl.BlockSpec((1, TILE, share), lambda i, m: (k, i, 0)),
                pl.BlockSpec((share, count * width), everything),
            ],
        ),
        out_shape=[
            jax.ShapeDtypeStruct((supernodes, rows, share), f32),
            jax.ShapeDtypeStruct((share, count * width), f32),
        ],
        input_output_aliases=aliases,
        compiler_params=pltpu.CompilerParams(vmem_limit_bytes=VMEM),
        cost_estimate=pl.CostEstimate(flops=FEED_COST, bytes_accessed=0, transcendentals=0),
    )(meta, *operands)


def around(pieces, col_number):
    size = len(pieces)
    ring = jnp.stack(pieces[::-1] + pieces[:0:-1])
    return lax.dynamic_slice_in_dim(ring, size - 1 - col_number, size, 0)


def row_sum_half(value, lane, row_size, gates=()):
    half = value.shape[0] // 2
    keep = lax.dynamic_slice_in_dim(value, lane * half, half, 0)
    give = lax.dynamic_slice_in_dim(value, (1 - lane) * half, half, 0)
    stages = [keep + swap(give, 1, row_size)]
    bit = 2
    while bit < row_size:
        value = stages[-1]
        if len(stages) <= len(gates):
            value = after(value, *gates[len(stages) - 1])
        stages.append(value + swap(value, bit, row_size))
        bit *= 2
    return stages


def both_halves(half, lane, row_size, axis):
    other = swap(half, 1, row_size)
    pick = lane == 0
    return jnp.concatenate(
        [jnp.where(pick, half, other), jnp.where(pick, other, half)], axis=axis
    )


def after(value, *others):
    return lax.optimization_barrier((value, *others))[0]


def own_blocks(meta, row, rows):
    block = min(rows, TILE)
    return [(at, block, meta[HEAD + (row + at) // TILE]) for at in range(0, rows, block)]


def feed_kernel(spots, meta, *refs):
    ways = len(spots)
    own, outs = refs[:ways], refs[-ways:]
    arrived = refs[ways:-ways]
    for way, row in enumerate(spots):
        out = outs[way]

        def fill(way=way, row=row, out=out):
            for at, block, flag in own_blocks(meta, row, out.shape[0]):
                value = own[way][0, at : at + block, :]
                out[at : at + block, :] = jnp.where(flag > 0, value, jnp.zeros_like(value))

        if not arrived:
            fill()
        else:
            first = meta[2 + way] == 0
            pl.when(first)(fill)

            @pl.when(jnp.logical_not(first))
            def _(way=way, out=out):
                out[...] = arrived[way][...]


def feed(meta, panels, k, stream, arrived):
    _, rows, width = panels.shape
    ways = 2
    piece = rows // (ways * STREAMS)
    block = pl.BlockSpec((piece, width), lambda i, m: (0, 0))
    return pl.pallas_call(
        functools.partial(feed_kernel, [(stream * ways + way) * piece for way in range(ways)]),
        grid_spec=pltpu.PrefetchScalarGridSpec(
            num_scalar_prefetch=1,
            grid=(1,),
            in_specs=[
                pl.BlockSpec((1, piece, width), lambda i, m, w=w: (k, stream * ways + w, 0))
                for w in range(ways)
            ]
            + [block] * len(arrived),
            out_specs=[block] * ways,
        ),
        out_shape=[jax.ShapeDtypeStruct((piece, width), bf16)] * ways,
        compiler_params=pltpu.CompilerParams(vmem_limit_bytes=VMEM),
        cost_estimate=pl.CostEstimate(flops=FEED_COST, bytes_accessed=0, transcendentals=0),
    )(meta, *[panels] * ways, *arrived)


def pick_kernel(k, spots, meta, panels, *refs):
    ways = len(spots)
    out, sems = refs[-2:]
    turns = len(refs[:-2]) // ways
    piece = out.shape[0] // ways

    def each(act):
        for way, row in enumerate(spots):
            base = way * piece
            turn = meta[2 + way]
            for t in range(turns):

                @pl.when(turn == t + 1)
                def _(way=way, t=t, base=base):
                    target = out.at[pl.ds(base, piece)]
                    act(pltpu.make_async_copy(refs[way * turns + t], target, sems.at[way, 0]))

            for n, (at, block, flag) in enumerate(own_blocks(meta, row, piece)):
                target = out.at[pl.ds(base + at, block)]

                @pl.when((turn == 0) & (flag > 0))
                def _(way=way, n=n, row=row, at=at, block=block, target=target):
                    source = panels.at[k, pl.ds(row + at, block)]
                    act(pltpu.make_async_copy(source, target, sems.at[way, n]))


    each(lambda copy: copy.start())
    for way, row in enumerate(spots):
        for at, block, flag in own_blocks(meta, row, piece):

            @pl.when((meta[2 + way] == 0) & (flag == 0))
            def _(at=way * piece + at, block=block):
                out[at : at + block, :] = jnp.zeros((block, out.shape[1]), out.dtype)

    each(lambda copy: copy.wait())


def pick(meta, panels, k, stream, received):
    _, rows, width = panels.shape
    ways = len(received)
    piece = rows // (ways * STREAMS)
    block = min(piece, TILE)
    operands = [panels] + [value for way in received for value in way]
    return pl.pallas_call(
        functools.partial(pick_kernel, k, [(stream * ways + way) * piece for way in range(ways)]),
        grid_spec=pltpu.PrefetchScalarGridSpec(
            num_scalar_prefetch=1,
            grid=(1,),
            in_specs=[pl.BlockSpec(memory_space=pltpu.HBM)] * len(operands),
            out_specs=pl.BlockSpec((ways * piece, width), lambda i, m: (0, 0)),
            scratch_shapes=[pltpu.SemaphoreType.DMA((ways, piece // block))],
        ),
        out_shape=jax.ShapeDtypeStruct((ways * piece, width), bf16),
        compiler_params=pltpu.CompilerParams(vmem_limit_bytes=VMEM),
    )(meta, *operands)


def send_on(values, orders, step, supernodes):
    size = len(orders[0])
    got = []
    for value, order in zip(values, orders):
        pairs = []
        for t in range(size - 1):
            if 0 <= step - t < supernodes:
                for c in range(size):
                    for i in range(LANES):
                        source = ((c ^ order[t]) * LANES + i) * size + c
                        target = ((c ^ order[t + 1]) * LANES + i) * size + c
                        pairs.append((source, target))
        got.append(lax.ppermute(value, BOTH, pairs))
    return got


def local(inverse_block, tile_list, panels, links, diag_inverse):
    rows_here = inverse_block.shape[0]
    share = diag_inverse.shape[2]
    row_size, col_size = lax.axis_size("row"), lax.axis_size("col")
    row_number, col_number = lax.axis_index("row"), lax.axis_index("col")
    place, lane = row_number // LANES, row_number % LANES
    supernodes, _, width = panels.shape
    tiles_here = rows_here // TILE
    tiles = row_number * tiles_here + jnp.arange(tiles_here, dtype=jnp.int32)
    flags = jnp.any(tile_list[None, :] == tiles[:, None], axis=1)

    order = [t ^ (t >> 1) for t in range(col_size)]
    back = [order[-t] for t in range(col_size)]
    orders = (order, back)
    relative = place ^ col_number
    turn = sum(jnp.where(relative == order[t], t, 0) for t in range(col_size))
    meta = jnp.concatenate(
        [
            jnp.stack([lane, col_number, turn, (col_size - turn) % col_size]).astype(jnp.int32),
            flags.astype(jnp.int32),
        ]
    )

    cross_parts, diag_parts = [], []
    carried = cross = stacked = full_turned = None
    link_full = None
    events = []
    steps = supernodes + col_size - 2
    parts, products, hops, sums, summed = [], [], [], [], []
    done = 0

    picked = []

    def finish(k, ties=(), gates=()):
        nonlocal carried
        right, left = hops[k][-1]
        if ties:
            right = after(right, *ties)
        if len(sums) <= k:
            carried, total = sum_parts(meta, parts[k], right, left, panels, k, carried)
            sums.append(total)
        total = sums[k]
        if gates is not None:
            summed.append(row_sum_half(total, lane, row_size, gates))

    def scatter(k):
        right, left = hops[k][-1]
        for hop in range(col_size // 2 - 1, 0, -1):
            right = after(right, products[-1], *(sums[-1:] if k == supernodes - 1 else []))
            right, left = pass_on(meta, parts[k], right, left, hop)
            hops[k].append((right, left))
            right, left = shift(right, 1, col_size), shift(left, -1, col_size)
            hops[k].append((right, left))

    def pick_now(q):
        k, stream = q // 2, q % 2
        flat = [
            events[2 * (k + t - 1) + stream][way] for way in range(2) for t in range(1, col_size)
        ]
        gate = [products[max(q - 2, min(q - 1, 1))]] if q > 0 else []
        flat = lax.optimization_barrier((*flat, *gate))
        own = pick(
            meta, panels, k, stream, [flat[: col_size - 1], flat[col_size - 1 : 2 * (col_size - 1)]]
        )
        picked.append((own, swap(own, 1, row_size)))

    def arrive(n):
        nonlocal done
        while done < 2 * supernodes:
            need = min(done + 1, 2 * supernodes - 1) if done > 1 else done
            if 2 * (need // 2 + col_size - 2) + need % 2 > n:
                break
            while len(picked) <= need:
                pick_now(len(picked))
            k, stream = done // 2, done % 2
            own, oth = picked[done]
            if need > done:
                own = after(own, *[pair[0] for pair in picked[done + 1 : need + 1]])
            link = None if k == 0 else link_full[k - 1]
            ties = products[-1:] or [link_full]
            if k == supernodes - 1 and k > 1:
                ties = ties + ([sums[0]] if stream == 0 else summed[0][:2])
            if ties:
                own = after(own, *ties)
            if stream == 0:
                products.append(panel_first(meta, inverse_block, own, oth))
            else:
                part, right, left = panel_second(
                    meta, inverse_block, own, oth, products[-1], link,
                    parts[-1] if k > 0 else None, col_size,
                )
                parts.append(part)
                products.append(part)
                hops.append([(shift(right, 1, col_size), shift(left, -1, col_size))])
            for k in range(supernodes):
                if done == min(2 * k + 2, 2 * supernodes - 1):
                    if k == supernodes - 1 > 1:
                        for earlier in range(1, k):
                            finish(earlier, products[-1:], None)
                    scatter(k)
            if done == 3 and supernodes > 2:
                finish(0, products[-1:])
            done += 1

    for step in range(steps):
        for stream in range(STREAMS):
            arrived = events[-STREAMS] if step > 0 else []
            if step < supernodes:
                values = feed(meta, panels, step, stream, arrived)
            else:
                values = arrived
            tie = events[-STREAMS - 1] if len(events) > STREAMS else []
            if len(events) == 2 * col_size - 1:
                tie = tie + products[:1]
            elif len(events) == 2 * col_size + 1:
                tie = tie + products[1:2]
            values = lax.optimization_barrier((*values, *tie))[: len(orders)]
            events.append(send_on(values, orders, step, supernodes))
            if len(events) == 2:
                flat = after(links, *events[0]).reshape(-1, width)
                half = flat.shape[0] // 2
                my_links = lax.dynamic_slice_in_dim(flat, lane * half, half, 0)
                got = around([my_links] + [shift(my_links, s, col_size) for s in range(1, col_size)], col_number)
                link_full = both_halves(got, lane, row_size, 1)
                link_full = link_full.reshape(col_size, supernodes - 1, -1, width)
                link_full = link_full.transpose(1, 0, 2, 3).reshape(supernodes - 1, width, width)
            arrive(len(events) - 1)
    for k in range(supernodes):
        last = k + 1 == supernodes
        if k == 0:
            for later in range(1, supernodes):
                if later + 1 < supernodes:
                    stages = hops[-1]
                    finish(later, (), ((), stages[-1]))
                else:
                    finish(later)
        link = None if k == 0 else link_full[k - 1]
        total = summed[k][-1]
        mine = lax.dynamic_slice_in_dim(diag_inverse[k], lane * (share // 2), share // 2, 1).T
        turned = mine - total[:, :width]
        if k > 0:
            link_wide = link.astype(f32)
            link_share = lax.dynamic_slice_in_dim(link_wide, col_number * share, share, 1)
            cross = -(stacked + turned_product(full_turned, link_share))
            cross_parts.append(cross)
            cross_half = lax.dynamic_slice_in_dim(cross, lane * (share // 2), share // 2, 1)
            turned = turned - turned_product(cross_half, link_wide)
        if last:
            diag_parts.append(both_halves(turned, lane, row_size, 0).T)
        else:
            arrived = []
            for s in range(col_size):
                at = (col_number + s) % col_size * share
                block = lax.dynamic_slice_in_dim(total[:, width:], at, share, 1)
                message = jnp.concatenate([turned, block], axis=1)
                arrived.append(shift(message, s, col_size) if s else message)
            if k + 2 < supernodes:
                arrived = after(tuple(arrived), sums[-1])
            ordered = around(list(arrived), col_number)
            ordered = both_halves(ordered, lane, row_size, 1)
            full_turned = ordered[:, :, :width].reshape(width, width)
            stacked = ordered[:, :, width:].reshape(width, share)
            diag_parts.append(
                lax.dynamic_slice_in_dim(full_turned, col_number * share, share, 0).T
            )
    return carried, jnp.stack(cross_parts), jnp.stack(diag_parts)


def solution(mesh):
    in_specs = (
        P("row", "col"),
        P(),
        P(None, "row", None),
        P(None, "col", None),
        P(None, None, "col"),
    )
    out_specs = (P(None, "row", "col"), P(None, None, "col"), P(None, None, "col"))
    return jax.shard_map(local, mesh=mesh, in_specs=in_specs, out_specs=out_specs, check_vma=False)
```
